128 devices in a mesh: row: 8 (over y_lo, z), col: 16 (over x, y_hi, core).
Axes of the slice: x: 4, y: 4 (y_hi: 2, y_lo: 2; y = y_hi * 2 + y_lo), z: 4, core: 2. Of those that a mesh axis runs over, the one named last changes fastest.
Arguments:
- carried_sum: float32 [7680, 28672], P('row', 'col'), may hold values from -6 to 6
- x_panels: bfloat16 [7680, 4096], P('row', 'col'), may hold values from -6 to 6
- w_panels: bfloat16 [4096, 28672], P('row', 'col'), may hold values from -0.0625 to 0.0625
- cotangent: bfloat16 [7680, 28672], P('row', 'col'), may hold values from -6 to 6
Outputs:
- activated: bfloat16 [7680, 28672], P('row', 'col')
- input_grad: bfloat16 [7680, 4096], P('row', 'col')
The draws below stay inside these ranges and needn't reach their ends.
All inputs are finite; a program needn't handle non-finite values.
Results may differ from the reference program's by a relative error of at most 0.017.
Values may be sent and summed in bfloat16 or wider, within the bound.
No kernel may reach another device: no remote copies, remote signals or barrier semaphores. Data moves between devices by JAX's collectives and lax.ppermute only.
A program may use at most 128 MiB of HBM per device.

```python
import jax
import jax.numpy as jnp
from jax import lax

D = 8192
FF = 28672
K = 4096
TOKENS = 7680
N_COL = 16


def block_scale(own_key, extent, split, least, high):
    factor_of, own = 1.0, jax.random.fold_in(own_key, 6)
    for axis_at, parts in split:
        heights = jnp.exp(jax.random.uniform(jax.random.fold_in(own, axis_at), (parts,), jnp.float32, least / len(split), high / len(split)))
        factor_of = factor_of * jnp.repeat(heights, extent[axis_at] // parts).reshape([-1 if axis == axis_at else 1 for axis in range(len(extent))])
    return factor_of


def centred(stream_key, extent, width, reach, cuts=(), dtype=jnp.bfloat16):
    result = jax.random.normal(stream_key, extent, jnp.float32) * width
    if len(cuts) > 0:
        result = block_scale(stream_key, extent, cuts, -0.22, 0.18) * result
    return jnp.clip(result, min=-reach, max=reach).astype(dtype)


def setup_inputs(seed: int = 0) -> dict:
    arg_keys = jax.random.split(jax.random.key(seed), 5)
    return {
        "carried_sum": centred(arg_keys[0], (TOKENS, FF), 1.0, 6.0, ((0, 8), (1, 16)), jnp.float32),
        "x_panels": centred(arg_keys[1], (TOKENS, K), 1.0, 6.0, ((0, 8), (1, 16))),
        "w_panels": centred(arg_keys[2], (K, FF), D ** -0.5, 0.0625, ((0, 8), (1, 16))),
        "cotangent": centred(arg_keys[3], (TOKENS, FF), 1.0, 6.0, ((0, 8), (1, 16))),
    }


inv_root_two = 0.7071067811865476
inv_root_tau = 0.3989422804014327


def reference(carried_sum, x_panels, w_panels, cotangent):
    preact = carried_sum + jnp.dot(x_panels, w_panels, preferred_element_type=jnp.float32)
    normal_cdf = 0.5 * (1.0 + jax.scipy.special.erf(preact * inv_root_two))
    normal_pdf = jnp.exp(-0.5 * preact * preact) * inv_root_tau
    activated = (preact * normal_cdf).astype(jnp.bfloat16)
    slope_grad = (cotangent.astype(jnp.float32) * (normal_cdf + preact * normal_pdf)).astype(jnp.bfloat16)
    block_width = FF // N_COL
    slope_blocks = jnp.transpose(slope_grad.reshape(TOKENS, N_COL, block_width), (1, 0, 2))
    weight_blocks = jnp.transpose(w_panels.reshape(K, N_COL, block_width), (1, 0, 2))

    def add_block(total, pair):
        slope_part, weight_part = pair
        partial_c = lax.dot_general(slope_part, weight_part, (((1,), (1,)), ((), ())), preferred_element_type=jnp.float32)
        return total + partial_c.astype(jnp.bfloat16).astype(jnp.float32), None

    input_grad, unused = lax.scan(add_block, jnp.zeros((TOKENS, K), jnp.float32), (slope_blocks, weight_blocks))
    return activated, input_grad.astype(jnp.bfloat16)
```

```python
import jax
import jax.numpy as jnp
from jax import lax
from jax.experimental import pallas as pl
from jax.experimental.pallas import tpu as pltpu
from jax.sharding import Mesh, PartitionSpec as P

inv_root_two = 0.7071067811865476
inv_root_tau = 0.3989422804014327

NZ, NX = 4, 4
WIDTHS = (1280, 512)
ROWS_AXES = ("y_lo", "z")
COLS_AXES = ("x", "y_hi", "core")
F32, BF16 = jnp.float32, jnp.bfloat16


def shift(value, axis, by, size):
    return lax.ppermute(value, axis, [(i, (i + by) % size) for i in range(size)])


def gather_w(own):
    half = own.shape[0] // 2
    z_minus = shift(own, "z", 1, NZ)
    z_plus = shift(own, "z", -1, NZ)
    other = shift(own, "y_lo", 1, 2)
    far_a = shift(z_minus[:half], "z", 1, NZ)
    far_b = shift(z_plus[half:], "z", -1, NZ)
    other_minus = shift(other, "z", 1, NZ)
    other_plus = shift(other, "z", -1, NZ)
    far = jnp.concatenate([far_a, far_b])
    other_far = shift(far, "y_lo", 1, 2)
    return jnp.stack([own, z_plus, far, z_minus, other, other_plus, other_far, other_minus])


def gather_x(own):
    pair = jnp.stack([own, shift(own, "y_hi", 1, 2)])
    x_minus = shift(pair, "x", 1, NX)
    x_plus = shift(pair, "x", -1, NX)
    far = jnp.stack([shift(x_minus[0], "x", 1, NX), shift(x_plus[1], "x", -1, NX)])
    mine = jnp.concatenate([pair, x_plus, far, x_minus])
    theirs = shift(mine, "core", 1, 2)
    return mine, theirs


def grad_kernel(pick_ref, core_ref, s_ref, w_ref, base_ref, mine_ref, theirs_ref):
    core = core_ref[0]
    rows = w_ref.shape[1] // 2
    for half, out in ((core, mine_ref), (1 - core, theirs_ref)):
        part = w_ref[0, pl.ds(pl.multiple_of(half * rows, rows), rows), :]
        out[0] = lax.dot_general(
            s_ref[...], part, (((1,), (1,)), ((), ())), preferred_element_type=F32
        ).astype(out.dtype)


def grad_blocks(s, w, picks, core, out_dtype):
    tokens, width = s.shape
    n = picks.shape[0]
    rows = w.shape[1]
    return pl.pallas_call(
        lambda p, c, a, b, m, t: grad_kernel(p, c, a, b, None, m, t),
        grid_spec=pltpu.PrefetchScalarGridSpec(
            num_scalar_prefetch=2,
            grid=(n,),
            in_specs=[
                pl.BlockSpec((tokens, width), lambda i, p, c: (0, 0)),
                pl.BlockSpec((1, rows, width), lambda i, p, c: (p[i], 0, 0)),
            ],
            out_specs=[
                pl.BlockSpec((1, tokens, rows // 2), lambda i, p, c: (i, 0, 0)),
                pl.BlockSpec((1, tokens, rows // 2), lambda i, p, c: (i, 0, 0)),
            ],
        ),
        out_shape=[jax.ShapeDtypeStruct((n, tokens, rows // 2), out_dtype)] * 2,
        compiler_params=pltpu.CompilerParams(vmem_limit_bytes=40 * 2**20),
        cost_estimate=pl.CostEstimate(flops=1000, bytes_accessed=1000, transcendentals=0),
    )(picks, core, s, w)


def body(carried_sum, x_panels, w_panels, cotangent):
    y_lo, z = lax.axis_index("y_lo"), lax.axis_index("z")
    x, y_hi, core = lax.axis_index("x"), lax.axis_index("y_hi"), lax.axis_index("core")
    core_of = core.reshape(1).astype(jnp.int32)

    which = []
    for dy in range(2):
        for dz in range(NZ):
            r = ((y_lo + dy) % 2) * NZ + (z + dz) % NZ
            which.append(((r // 2 - x) % NX) * 2 + (r % 2 - y_hi) % 2)

    def block_for(dx, dyh):
        r = ((x + dx) % NX) * 2 + (y_hi + dyh) % 2
        return ((r // NZ - y_lo) % 2) * NZ + (r % NZ - z) % NZ

    order = ((2, 0), (2, 1), (1, 1), (3, 1), (1, 0), (3, 0), (0, 1), (0, 0))
    picks = jnp.stack([block_for(*d) for d in order]).astype(jnp.int32)

    mine, theirs = gather_x(x_panels)
    first = jnp.where(core == 0, mine, theirs)
    second = jnp.where(core == 0, theirs, mine)
    x_cols = []
    for at in which:
        x_cols.append(lax.dynamic_index_in_dim(first, at, 0, keepdims=False))
        x_cols.append(lax.dynamic_index_in_dim(second, at, 0, keepdims=False))
    x_whole = jnp.concatenate(x_cols, axis=1)

    activated, grads = [], []
    start = 0
    w_chunks, s_chunks = [], []
    for width in WIDTHS:
        cols = slice(start, start + width)
        start += width
        w_all = gather_w(w_panels[:, cols])
        preact = carried_sum[:, cols] + jnp.dot(
            x_whole, w_all.reshape(-1, width), preferred_element_type=F32
        )
        normal_cdf = 0.5 * (1.0 + jax.scipy.special.erf(preact * inv_root_two))
        normal_pdf = jnp.exp(-0.5 * preact * preact) * inv_root_tau
        activated.append((preact * normal_cdf).astype(BF16))
        s_chunks.append(
            (cotangent[:, cols].astype(F32) * (normal_cdf + preact * normal_pdf)).astype(BF16)
        )
        w_chunks.append(w_all)

    base_mine, base_theirs = grad_blocks(s_chunks[0], w_chunks[0], picks, core_of, F32)

    def blocks(lo, hi):
        m, t = grad_blocks(s_chunks[1], w_chunks[1], picks[lo:hi], core_of, F32)
        m = m + base_mine[lo:hi]
        t = (t + base_theirs[lo:hi]).astype(BF16)
        return m + shift(t, "core", 1, 2).astype(F32)

    half = carried_sum.shape[0] // 2
    b2 = blocks(0, 2).astype(BF16)
    via_minus = shift(b2[:, :half], "x", 1, NX)
    via_plus = shift(b2[:, half:], "x", -1, NX)
    got = []
    for pair in (1, 0):
        b13 = blocks(2, 4) if pair == 1 else blocks(4, 6)
        up = jnp.concatenate([b13[0, :half] + via_minus[pair].astype(F32), b13[0, half:]])
        down = jnp.concatenate([b13[1, :half], b13[1, half:] + via_plus[pair].astype(F32)])
        got.append(
            (shift(up.astype(BF16), "x", 1, NX), shift(down.astype(BF16), "x", -1, NX))
        )
    b0 = blocks(6, 8)
    to_other = b0[0] + got[0][0].astype(F32) + got[0][1].astype(F32)
    from_other = shift(to_other.astype(BF16), "y_hi", 1, 2)
    input_grad = (
        b0[1] + got[1][0].astype(F32) + got[1][1].astype(F32) + from_other.astype(F32)
    ).astype(BF16)
    return jnp.concatenate(activated, axis=1), input_grad


def solution(mesh):
    fine = Mesh(mesh.devices.reshape(2, 4, 4, 2, 2), ROWS_AXES + COLS_AXES)
    spec = P(ROWS_AXES, COLS_AXES)
    return jax.shard_map(
        body,
        mesh=fine,
        in_specs=(spec, spec, spec, spec),
        out_specs=(spec, spec),
        check_vma=False,
    )
```

```python
import jax
import jax.numpy as jnp
from jax import lax
from jax.experimental import pallas as pl
from jax.experimental.pallas import tpu as pltpu
from jax.sharding import Mesh, PartitionSpec as P

inv_root_two = 0.7071067811865476
inv_root_tau = 0.3989422804014327

NZ, NX = 4, 4
LANES = 256
WIDTH_A = 1280
ROWS_AXES = ("y_lo", "z")
COLS_AXES = ("x", "y_hi", "core")
F32, BF16 = jnp.float32, jnp.bfloat16
VMEM_LIMIT = 62 * 2**20
PARTS = 2


CHEAP = pl.CostEstimate(flops=1000, bytes_accessed=1000, transcendentals=0)


def flops(n):
    return pl.CostEstimate(flops=n, bytes_accessed=1000, transcendentals=0)


DEAR = flops(4 * 10**10)


def shift(value, axis, by, size):
    pairs = [(i, (i + by) % size) for i in range(size)]
    return lax.ppermute(value, axis, pairs)


def after(value, *deps):
    return lax.optimization_barrier((value, *deps))[0]


def forward_early(places, late, core, mine, theirs, start, shards):
    tokens, width = start.shape
    panels = sum(p.shape[0] for p in mine)
    n, n_p, n_late = len(shards), len(mine), late.shape[0]
    rows = shards[0][0].shape[0]
    pieces = [a for shard in shards for a in shard]

    def kernel(places_ref, late_ref, core_ref, *refs):
        parts, (start_ref, *refs) = refs[: 2 * n_p], refs[2 * n_p :]
        w_refs = refs[: len(pieces)]
        total_ref, late_x_ref, mine_ref, theirs_ref, sems, late_sems = refs[len(pieces) :]
        i = pl.program_id(0)
        own = core_ref[0]
        out_copies = []
        for j in range(n_late):
            for k, buf in enumerate((mine_ref, theirs_ref)):
                column = pl.multiple_of((2 * j + jnp.where(own == k, 0, 1)) * LANES, LANES)
                out_copies.append(
                    pltpu.make_async_copy(
                        buf.at[late_ref[j]],
                        late_x_ref.at[:, pl.ds(column, LANES)],
                        late_sems.at[2 * j + k],
                    )
                )

        @pl.when(i == 0)
        def _():
            copies = []
            for k, buf in enumerate((mine_ref, theirs_ref)):
                to = 0
                for part in parts[k * n_p : (k + 1) * n_p]:
                    held = buf.at[pl.ds(to, part.shape[0])]
                    copies.append(pltpu.make_async_copy(part, held, sems.at[len(copies)]))
                    to += part.shape[0]
            for c in copies:
                c.start()
            for c in copies:
                c.wait()
            for c in out_copies:
                c.start()

        lo = pl.multiple_of(own * LANES, LANES)
        hi = pl.multiple_of((1 - own) * LANES, LANES)
        lhs = jnp.concatenate(
            [r[places_ref[j]] for j in range(n) for r in (mine_ref, theirs_ref)], axis=1
        )
        rhs, at = [], 0
        for shard in shards:
            held = w_refs[at : at + len(shard)]
            for o in (lo, hi):
                block = held[0][pl.ds(o, LANES), :]
                if len(shard) == 2:
                    edge = shard[0].shape[1] // LANES
                    block = jnp.where(i < edge, block, held[1][pl.ds(o, LANES), :])
                rhs.append(block)
            at += len(shard)
        rhs = jnp.concatenate(rhs, axis=0)
        total_ref[...] = start_ref[...] + jnp.dot(lhs, rhs, preferred_element_type=F32)

        @pl.when(i == pl.num_programs(0) - 1)
        def _():
            for c in out_copies:
                c.wait()

    def piece_specs(shard):
        if len(shard) == 1:
            return [pl.BlockSpec((rows, LANES), lambda i, *_: (0, i))]
        edge = shard[0].shape[1] // LANES
        return [
            pl.BlockSpec((rows, LANES), lambda i, *_: (0, jnp.minimum(i, edge - 1))),
            pl.BlockSpec((rows, LANES), lambda i, *_: (0, jnp.maximum(i - edge, 0))),
        ]

    tile = pl.BlockSpec((tokens, LANES), lambda i, *_: (0, i))
    hbm = pl.BlockSpec(memory_space=pl.ANY)
    return pl.pallas_call(
        kernel,
        grid_spec=pltpu.PrefetchScalarGridSpec(
            num_scalar_prefetch=3,
            grid=(width // LANES,),
            in_specs=[hbm] * (2 * n_p) + [tile] + [p for shard in shards for p in piece_specs(shard)],
            out_specs=[tile, hbm],
            scratch_shapes=[pltpu.VMEM((panels, tokens, LANES), BF16)] * 2
            + [pltpu.SemaphoreType.DMA((2 * n_p,)), pltpu.SemaphoreType.DMA((2 * n_late,))],
        ),
        out_shape=[
            jax.ShapeDtypeStruct((tokens, width), F32),
            jax.ShapeDtypeStruct((tokens, 2 * n_late * LANES), BF16),
        ],
        compiler_params=pltpu.CompilerParams(vmem_limit_bytes=VMEM_LIMIT),
        cost_estimate=CHEAP,
        name="early",
    )(places, late, core, *mine, *theirs, start, *pieces)


def forward_late(late_x, total, cotangent, shards, offset, dest, name):
    tokens, width = total.shape
    rows, cols = shards[0].shape
    n = len(shards)
    depth = late_x.shape[1]
    t = tokens // PARTS

    def kernel(x_ref, start_ref, cot_ref, *refs):
        w_refs, (act_ref, slope_ref) = refs[:n], refs[-2:]
        rhs = jnp.concatenate([w[...] for w in w_refs], axis=0)
        for p in range(PARTS):
            at = pl.ds(p * t, t)
            preact = start_ref[at, :] + jnp.dot(x_ref[at, :], rhs, preferred_element_type=F32)
            normal_cdf = 0.5 * (1.0 + lax.erf(preact * inv_root_two))
            normal_pdf = jnp.exp(-0.5 * preact * preact) * inv_root_tau
            act_ref[at, :] = (preact * normal_cdf).astype(BF16)
            slope = cot_ref[at, :].astype(F32) * (normal_cdf + preact * normal_pdf)
            slope_ref[at, :] = slope.astype(BF16)

    first = offset // LANES
    tile = pl.BlockSpec((tokens, LANES), lambda i: (0, i + first))
    return pl.pallas_call(
        kernel,
        grid=(cols // LANES,),
        in_specs=[pl.BlockSpec((tokens, depth), lambda i: (0, 0)), tile, tile]
        + [pl.BlockSpec((rows, LANES), lambda i: (0, i))] * n
        + [pl.BlockSpec(memory_space=pl.ANY)] * len(dest),
        out_specs=[tile, tile],
        out_shape=[jax.ShapeDtypeStruct((tokens, width), BF16)] * 2,
        input_output_aliases={3 + n + k: k for k in range(len(dest))},
        compiler_params=pltpu.CompilerParams(vmem_limit_bytes=VMEM_LIMIT),
        cost_estimate=CHEAP,
        name=name,
    )(late_x, total, cotangent, *shards, *dest)


def gradient(picks, core, slope, blocks, name):
    tokens, width = slope.shape
    rows = 2 * LANES
    n = picks.shape[0]
    arrays = [a for shard in blocks for a in shard]

    def kernel(picks_ref, core_ref, s_ref, *refs):
        a_refs, (mine_ref, theirs_ref, w_buf, sem) = refs[: len(arrays)], refs[len(arrays) :]
        i = pl.program_id(0)

        def fetch(step, slot):
            wanted = picks_ref[step]
            at = 0
            for j, shard in enumerate(blocks):
                held = a_refs[at : at + len(shard)]
                at += len(shard)

                @pl.when(wanted == j)
                def _():
                    to = 0
                    for ref in held:
                        w = ref.shape[1]
                        pltpu.make_async_copy(
                            ref, w_buf.at[slot, :, pl.ds(to, w)], sem.at[slot]
                        ).start()
                        to += w

        @pl.when(i == 0)
        def _():
            fetch(0, 0)

        @pl.when(i + 1 < n)
        def _():
            fetch(i + 1, (i + 1) % 2)

        slot = i % 2
        pltpu.make_async_copy(a_refs[0], w_buf.at[slot], sem.at[slot]).wait()
        own = core_ref[0]
        for half, out in ((own, mine_ref), (1 - own, theirs_ref)):
            part = w_buf[slot, pl.ds(pl.multiple_of(half * LANES, LANES), LANES), :]
            out[0] = lax.dot_general(
                s_ref[...], part, (((1,), (1,)), ((), ())), preferred_element_type=F32
            ).astype(BF16)

    out_block = pl.BlockSpec((1, tokens, LANES), lambda i, *_: (i, 0, 0))
    return pl.pallas_call(
        kernel,
        grid_spec=pltpu.PrefetchScalarGridSpec(
            num_scalar_prefetch=2,
            grid=(n,),
            in_specs=[pl.BlockSpec((tokens, width), lambda i, *_: (0, 0))]
            + [pl.BlockSpec(memory_space=pl.ANY)] * len(arrays),
            out_specs=[out_block, out_block],
            scratch_shapes=[pltpu.VMEM((2, rows, width), BF16), pltpu.SemaphoreType.DMA((2,))],
        ),
        out_shape=[jax.ShapeDtypeStruct((n, tokens, LANES), BF16)] * 2,
        compiler_params=pltpu.CompilerParams(vmem_limit_bytes=VMEM_LIMIT),
        cost_estimate=CHEAP,
        name=name,
    )(picks, core, slope, *arrays)


def cut_first(z_minus, z_plus):
    rows, width = z_minus.shape
    steps = 4

    def kernel(minus_ref, plus_ref, up_ref, down_ref):
        up_ref[...] = minus_ref[...]
        down_ref[...] = plus_ref[...]

    def block(at=0):
        return pl.BlockSpec((rows // 2 // steps, width), lambda i: (i + at, 0))

    return pl.pallas_call(
        kernel,
        grid=(steps,),
        in_specs=[block(), block(steps)],
        out_specs=[block()] * 2,
        out_shape=[jax.ShapeDtypeStruct((rows // 2, width), BF16)] * 2,
        cost_estimate=DEAR,
        name="cut_first",
    )(z_minus, z_plus)


def cut_far(far_a, far_b, width_a):
    half, width = far_a.shape

    def kernel(top_ref, low_ref, a_ref, b_ref):
        for k, ref in enumerate((top_ref, low_ref)):
            at = pl.ds(k * half, half)
            a_ref[at, :] = ref[:, :width_a]
            b_ref[at, :] = ref[:, width_a:]

    return pl.pallas_call(
        kernel,
        out_shape=[jax.ShapeDtypeStruct((2 * half, w), BF16) for w in (width_a, width - width_a)],
        cost_estimate=CHEAP,
        name="cut_far",
    )(far_a, far_b)


def mark(cost, *arrays):
    n = len(arrays)
    any_space = [pl.BlockSpec(memory_space=pl.ANY)] * n
    return pl.pallas_call(
        lambda *refs: None,
        in_specs=any_space,
        out_specs=any_space,
        out_shape=[jax.ShapeDtypeStruct(a.shape, a.dtype) for a in arrays],
        input_output_aliases={i: i for i in range(n)},
        cost_estimate=cost,
        name="mark",
    )(*arrays)


def add_up(mine, back, via_minus, via_plus, dyh, name):
    tokens, lanes = mine.shape[1:]
    steps = 2
    t = tokens // steps

    def kernel(mine_ref, back_ref, minus_ref, plus_ref, up_ref, down_ref, own_ref):
        first = pl.program_id(0) < steps // 2
        total = mine_ref[...].astype(F32) + back_ref[...].astype(F32)
        minus, plus = minus_ref[0].astype(F32), plus_ref[0].astype(F32)
        up_ref[...] = (total[0] + jnp.where(first, minus, 0.0)).astype(BF16)
        down_ref[...] = (total[1] + jnp.where(first, 0.0, plus)).astype(BF16)
        own_ref[...] = total[2]

    tile = pl.BlockSpec((t, lanes), lambda i: (i, 0))
    three = pl.BlockSpec((3, t, lanes), lambda i: (0, i, 0))
    last = steps // 2 - 1
    return pl.pallas_call(
        kernel,
        grid=(steps,),
        in_specs=[
            three,
            three,
            pl.BlockSpec((1, t, lanes), lambda i: (dyh, jnp.minimum(i, last), 0)),
            pl.BlockSpec((1, t, lanes), lambda i: (dyh, jnp.maximum(i - last - 1, 0), 0)),
        ],
        out_specs=[tile] * 3,
        out_shape=[jax.ShapeDtypeStruct((tokens, lanes), d) for d in (BF16, BF16, F32)],
        cost_estimate=CHEAP,
        name=name,
    )(mine, back, via_minus, via_plus)


def body(carried_sum, x_panels, w_panels, cotangent):
    y_lo, z = lax.axis_index("y_lo"), lax.axis_index("z")
    x, y_hi, core = lax.axis_index("x"), lax.axis_index("y_hi"), lax.axis_index("core")
    core_of = core.reshape(1).astype(jnp.int32)
    tokens, width = carried_sum.shape
    width_a, width_b = WIDTH_A, width - WIDTH_A
    rows = w_panels.shape[0]

    def panels_for(dy, dz):
        r = ((y_lo + dy) % 2) * NZ + (z + dz) % NZ
        dx = (r // 2 - x) % NX
        return (dx ^ (dx >> 1)) * 2 + (r % 2 - y_hi) % 2

    def places(*ds):
        return jnp.stack([panels_for(*d) for d in ds]).astype(jnp.int32)

    def block_for(dx, dyh):
        r = ((x + dx) % NX) * 2 + (y_hi + dyh) % 2
        return ((r // NZ - y_lo) % 2) * NZ + (r % NZ - z) % NZ

    def picks(*ds):
        return jnp.stack([block_for(*d) for d in ds]).astype(jnp.int32)

    w_a, w_b = w_panels[:, :width_a], w_panels[:, width_a:]
    z_minus = shift(w_panels, "z", 1, NZ)
    z_plus = shift(w_panels, "z", -1, NZ)
    other_a = shift(w_a, "y_lo", 1, 2)
    pair = mark(flops(38 * 10**9), jnp.stack([x_panels, shift(x_panels, "y_hi", 1, 2)]))[0]
    x_minus = shift(pair, "x", 1, NX)
    x_plus = shift(pair, "x", -1, NX)
    up, down = cut_first(z_minus, z_plus)
    other_a = mark(DEAR, other_a)[0]
    up, down, w_b, other_a, x_minus, x_plus = lax.optimization_barrier(
        (up, down, w_b, other_a, x_minus, x_plus)
    )
    far_top = shift(up, "z", 1, NZ)
    far_low = shift(down, "z", -1, NZ)
    near = jnp.concatenate([pair, x_plus, x_minus])
    near_theirs = shift(near, "core", 1, 2)
    other_b = shift(after(w_b, near_theirs), "y_lo", 1, 2)
    x_far = [shift(x_minus[0], "x", 1, NX), shift(x_plus[1], "x", -1, NX)]
    x_far = jnp.stack(x_far)
    mine = [near, x_far]
    theirs = [near_theirs, shift(x_far, "core", 1, 2)]
    far_a, far_b = cut_far(far_top, far_low, width_a)
    send_a = after(other_a, far_a, other_b)
    other_minus_a = shift(send_a, "z", 1, NZ)
    other_plus_a = shift(send_a, "z", -1, NZ)
    other_far_a = shift(far_a, "y_lo", 1, 2)
    total, late_x = forward_early(
        places((0, 0), (0, 1), (0, 3), (1, 0)),
        places((0, 2), (1, 1), (1, 3), (1, 2)),
        core_of, mine, theirs, carried_sum,
        [(w_panels,), (z_plus,), (z_minus,), (other_a, other_b)],
    )
    send_b, send_far_b = lax.optimization_barrier(
        (other_b, far_b, other_minus_a, other_plus_a, other_far_a, total)
    )[:2]
    other_minus_b = shift(send_b, "z", 1, NZ)
    other_plus_b = shift(send_b, "z", -1, NZ)
    other_far_b = shift(send_far_b, "y_lo", 1, 2)
    done = forward_late(
        late_x, total, cotangent, [far_a, other_plus_a, other_minus_a, other_far_a], 0, [], "gelu_a"
    )
    activated, slope = forward_late(
        late_x, total, cotangent, [far_b, other_plus_b, other_minus_b, other_far_b], width_a, done, "gelu_b"
    )
    blocks = [(w_panels,), (z_plus,), (far_a, far_b), (z_minus,), (other_a, other_b)]
    blocks += [(other_plus_a, other_plus_b), (other_far_a, other_far_b), (other_minus_a, other_minus_b)]

    half = tokens // 2
    m, t = gradient(picks((2, 0), (2, 1)), core_of, slope, blocks, "grad_far")
    far_sum = (m.astype(F32) + shift(t, "core", 1, 2).astype(F32)).astype(BF16)
    up, down = lax.optimization_barrier((far_sum[:, :half], far_sum[:, half:]))
    via_minus = shift(up, "x", 1, NX)
    via_plus = shift(down, "x", -1, NX)

    slope = after(slope, up, down)
    m, t = gradient(picks((1, 1), (3, 1), (0, 1)), core_of, slope, blocks, "grad_1")
    via_minus, via_plus = mark(DEAR, via_minus, via_plus)
    up, down, own_1 = add_up(m, shift(t, "core", 1, 2), via_minus, via_plus, 1, "add_1")
    got_1 = shift(up, "x", 1, NX), shift(down, "x", -1, NX)

    slope = after(slope, up, down)
    m, t = gradient(picks((1, 0), (3, 0), (0, 0)), core_of, slope, blocks, "grad_0")
    got_1 = mark(DEAR, *got_1)
    m, via_minus, *got_1 = lax.optimization_barrier((m, via_minus, *got_1))
    up, down, own_0 = add_up(m, shift(t, "core", 1, 2), via_minus, via_plus, 0, "add_0")
    got_0 = shift(up, "x", 1, NX), shift(down, "x", -1, NX)
    to_other = own_1 + got_1[0].astype(F32) + got_1[1].astype(F32)
    from_other = shift(to_other.astype(BF16), "y_hi", 1, 2)
    input_grad = own_0 + got_0[0].astype(F32) + got_0[1].astype(F32) + from_other.astype(F32)
    return activated, input_grad.astype(BF16)


def solution(mesh):
    fine = Mesh(mesh.devices.reshape(2, 4, 4, 2, 2), ROWS_AXES + COLS_AXES)
    spec = P(ROWS_AXES, COLS_AXES)
    return jax.shard_map(
        body,
        mesh=fine,
        in_specs=(spec, spec, spec, spec),
        out_specs=(spec, spec),
        check_vma=False,
    )
```

```python
import jax
import jax.numpy as jnp
from jax import lax
from jax.experimental import pallas as pl
from jax.experimental.pallas import tpu as pltpu
from jax.sharding import Mesh, PartitionSpec as P

inv_root_two = 0.7071067811865476
inv_root_tau = 0.3989422804014327

NZ, NX = 4, 4
LANES = 256
WIDTH_A = 1280
ROWS_AXES = ("y_lo", "z")
COLS_AXES = ("x", "y_hi", "core")
F32, BF16 = jnp.float32, jnp.bfloat16
VMEM_LIMIT = 62 * 2**20
SMALL_LIMIT = 16 * 2**20
PARTS = 2
CHUNKS = 2


CHEAP = pl.CostEstimate(flops=1000, bytes_accessed=1000, transcendentals=0)


def flops(n):
    return pl.CostEstimate(flops=n, bytes_accessed=1000, transcendentals=0)


DEAR = flops(4 * 10**10)


def shift(value, axis, by, size):
    pairs = [(i, (i + by) % size) for i in range(size)]
    return lax.ppermute(value, axis, pairs)


def after(value, *deps):
    return lax.optimization_barrier((value, *deps))[0]


def panel_place(dy, dz):
    r = ((lax.axis_index("y_lo") + dy) & 1) * NZ + ((lax.axis_index("z") + dz) & (NZ - 1))
    dx = ((r >> 1) - lax.axis_index("x")) & (NX - 1)
    return (dx ^ (dx >> 1)) * 2 + ((r ^ lax.axis_index("y_hi")) & 1)


def block_place(dx, dyh):
    r = ((lax.axis_index("x") + dx) & (NX - 1)) * 2 + ((lax.axis_index("y_hi") + dyh) & 1)
    return (((r >> 2) ^ lax.axis_index("y_lo")) & 1) * NZ + ((r - lax.axis_index("z")) & (NZ - 1))


def forward_early(early, late, mine, theirs, start, shards):
    tokens, width = start.shape
    panels = sum(p.shape[0] for p in mine)
    n, n_p, n_late = len(shards), len(mine) + len(theirs), len(late)
    rows = shards[0][0].shape[0]
    pieces = [a for shard in shards for a in shard]

    def kernel(*refs):
        parts, (start_ref, *refs) = refs[:n_p], refs[n_p:]
        w_refs = refs[: len(pieces)]
        total_ref, late_x_ref, mine_ref, theirs_ref, sems, late_sems = refs[len(pieces) :]
        i = pl.program_id(0)
        own = lax.axis_index("core")
        out_copies = []
        for j, spot in enumerate(late):
            place = panel_place(*spot)
            for k, buf in enumerate((mine_ref, theirs_ref)):
                column = pl.multiple_of((2 * j + jnp.where(own == k, 0, 1)) * LANES, LANES)
                out_copies.append(
                    pltpu.make_async_copy(
                        buf.at[place],
                        late_x_ref.at[:, pl.ds(column, LANES)],
                        late_sems.at[2 * j + k],
                    )
                )

        @pl.when(i == 0)
        def _():
            copies = []
            for buf, own_parts in ((mine_ref, parts[: len(mine)]), (theirs_ref, parts[len(mine) :])):
                to = 0
                for part in own_parts:
                    held = buf.at[pl.ds(to, part.shape[0])]
                    copies.append(pltpu.make_async_copy(part, held, sems.at[len(copies)]))
                    to += part.shape[0]
            for c in copies:
                c.start()
            for c in copies:
                c.wait()
            for c in out_copies:
                c.start()

        lo = pl.multiple_of(own * LANES, LANES)
        hi = pl.multiple_of((1 - own) * LANES, LANES)
        lhs = jnp.concatenate(
            [r[panel_place(*spot)] for spot in early for r in (mine_ref, theirs_ref)], axis=1
        )
        rhs, at = [], 0
        for shard in shards:
            held = w_refs[at : at + len(shard)]
            for o in (lo, hi):
                block = held[0][pl.ds(o, LANES), :]
                if len(shard) == 2:
                    edge = shard[0].shape[1] // LANES
                    block = jnp.where(i < edge, block, held[1][pl.ds(o, LANES), :])
                rhs.append(block)
            at += len(shard)
        rhs = jnp.concatenate(rhs, axis=0)
        total_ref[...] = start_ref[...] + jnp.dot(lhs, rhs, preferred_element_type=F32)

        @pl.when(i == pl.num_programs(0) - 1)
        def _():
            for c in out_copies:
                c.wait()

    def piece_specs(shard):
        if len(shard) == 1:
            return [pl.BlockSpec((rows, LANES), lambda i, *_: (0, i))]
        edge = shard[0].shape[1] // LANES
        return [
            pl.BlockSpec((rows, LANES), lambda i, *_: (0, jnp.minimum(i, edge - 1))),
            pl.BlockSpec((rows, LANES), lambda i, *_: (0, jnp.maximum(i - edge, 0))),
        ]

    tile = pl.BlockSpec((tokens, LANES), lambda i, *_: (0, i))
    hbm = pl.BlockSpec(memory_space=pl.ANY)
    return pl.pallas_call(
        kernel,
        grid=(width // LANES,),
        in_specs=[hbm] * n_p + [tile] + [p for shard in shards for p in piece_specs(shard)],
        out_specs=[tile, hbm],
        scratch_shapes=[pltpu.VMEM((panels, tokens, LANES), BF16)] * 2
        + [pltpu.SemaphoreType.DMA((n_p,)), pltpu.SemaphoreType.DMA((2 * n_late,))],
        out_shape=[
            jax.ShapeDtypeStruct((tokens, width), F32),
            jax.ShapeDtypeStruct((tokens, 2 * n_late * LANES), BF16),
        ],
        compiler_params=pltpu.CompilerParams(vmem_limit_bytes=VMEM_LIMIT),
        cost_estimate=CHEAP,
        name="early",
    )(*mine, *theirs, start, *pieces)


def forward_late(late_x, total, cotangent, shards, offset, dest, name):
    tokens, width = total.shape
    rows, cols = shards[0].shape
    n = len(shards)
    depth = late_x.shape[1]
    t = tokens // PARTS

    def kernel(x_ref, start_ref, cot_ref, *refs):
        w_refs, (act_ref, slope_ref) = refs[:n], refs[-2:]
        rhs = jnp.concatenate([w[...] for w in w_refs], axis=0)
        for p in range(PARTS):
            at = pl.ds(p * t, t)
            preact = start_ref[at, :] + jnp.dot(x_ref[at, :], rhs, preferred_element_type=F32)
            normal_cdf = 0.5 * (1.0 + lax.erf(preact * inv_root_two))
            normal_pdf = jnp.exp(-0.5 * preact * preact) * inv_root_tau
            act_ref[at, :] = (preact * normal_cdf).astype(BF16)
            slope = cot_ref[at, :].astype(F32) * (normal_cdf + preact * normal_pdf)
            slope_ref[at, :] = slope.astype(BF16)

    first = offset // LANES
    tile = pl.BlockSpec((tokens, LANES), lambda i: (0, i + first))
    return pl.pallas_call(
        kernel,
        grid=(cols // LANES,),
        in_specs=[pl.BlockSpec((tokens, depth), lambda i: (0, 0)), tile, tile]
        + [pl.BlockSpec((rows, LANES), lambda i: (0, i))] * n
        + [pl.BlockSpec(memory_space=pl.ANY)] * len(dest),
        out_specs=[tile, tile],
        out_shape=[jax.ShapeDtypeStruct((tokens, width), BF16)] * 2,
        input_output_aliases={3 + n + k: k for k in range(len(dest))},
        compiler_params=pltpu.CompilerParams(vmem_limit_bytes=VMEM_LIMIT),
        cost_estimate=CHEAP,
        name=name,
    )(late_x, total, cotangent, *shards, *dest)


def gradient(places, slope, blocks, name):
    tokens, width = slope.shape
    rows = 2 * LANES
    n = len(places)
    arrays = [a for shard in blocks for a in shard]
    t = tokens // CHUNKS

    def kernel(s_hbm, *refs):
        a_refs, refs = refs[: len(arrays)], refs[len(arrays) :]
        mine_hbm, theirs_hbm, s_buf, w_buf, out_buf, s_sem, w_sem, out_sem = refs

        def fetch(k):
            wanted = block_place(*places[k])
            at = 0
            for j, shard in enumerate(blocks):
                held = a_refs[at : at + len(shard)]
                at += len(shard)

                @pl.when(wanted == j)
                def _():
                    to = 0
                    for ref in held:
                        w = ref.shape[1]
                        pltpu.make_async_copy(ref, w_buf.at[k, :, pl.ds(to, w)], w_sem.at[k]).start()
                        to += w

        chunks = [pl.ds(c * t, t) for c in range(CHUNKS)]
        loads = [
            pltpu.make_async_copy(s_hbm.at[at], s_buf.at[at], s_sem.at[c]) for c, at in enumerate(chunks)
        ]
        fetch(0)
        for load in loads:
            load.start()
        own = lax.axis_index("core")
        stores = []
        for k in range(n):
            if k + 1 < n:
                fetch(k + 1)
            pltpu.make_async_copy(a_refs[0], w_buf.at[k], w_sem.at[k]).wait()
            for c, at in enumerate(chunks):
                if k == 0:
                    loads[c].wait()
                for h, (half, out) in enumerate(((1 - own, theirs_hbm), (own, mine_hbm))):
                    part = w_buf[k, pl.ds(pl.multiple_of(half * LANES, LANES), LANES), :]
                    out_buf[k, h, at, :] = lax.dot_general(
                        s_buf[at, :], part, (((1,), (1,)), ((), ())), preferred_element_type=F32
                    ).astype(BF16)
                    store = pltpu.make_async_copy(
                        out_buf.at[k, h, at], out.at[k, at], out_sem.at[k, h, c]
                    )
                    store.start()
                    stores.append(store)
        for store in stores:
            store.wait()

    hbm = pl.BlockSpec(memory_space=pl.ANY)
    return pl.pallas_call(
        kernel,
        in_specs=[hbm] * (1 + len(arrays)),
        out_specs=[hbm] * 2,
        scratch_shapes=[
            pltpu.VMEM((tokens, width), BF16),
            pltpu.VMEM((n, rows, width), BF16),
            pltpu.VMEM((n, 2, tokens, LANES), BF16),
            pltpu.SemaphoreType.DMA((CHUNKS,)),
            pltpu.SemaphoreType.DMA((n,)),
            pltpu.SemaphoreType.DMA((n, 2, CHUNKS)),
        ],
        out_shape=[jax.ShapeDtypeStruct((n, tokens, LANES), BF16)] * 2,
        compiler_params=pltpu.CompilerParams(vmem_limit_bytes=VMEM_LIMIT),
        cost_estimate=CHEAP,
        name=name,
    )(slope, *arrays)


def mark(cost, *arrays):
    n = len(arrays)
    any_space = [pl.BlockSpec(memory_space=pl.ANY)] * n
    return pl.pallas_call(
        lambda *refs: None,
        in_specs=any_space,
        out_specs=any_space,
        out_shape=[jax.ShapeDtypeStruct(a.shape, a.dtype) for a in arrays],
        input_output_aliases={i: i for i in range(n)},
        compiler_params=pltpu.CompilerParams(vmem_limit_bytes=SMALL_LIMIT),
        cost_estimate=cost,
        name="mark",
    )(*arrays)


def add_up(mine, back, via_minus, via_plus, dyh, name):
    tokens, lanes = mine.shape[1:]
    steps = 2
    t = tokens // steps

    def kernel(mine_ref, back_ref, minus_ref, plus_ref, up_ref, down_ref, own_ref):
        first = pl.program_id(0) < steps // 2
        total = mine_ref[...].astype(F32) + back_ref[...].astype(F32)
        minus, plus = minus_ref[0].astype(F32), plus_ref[0].astype(F32)
        up_ref[...] = (total[0] + jnp.where(first, minus, 0.0)).astype(BF16)
        down_ref[...] = (total[1] + jnp.where(first, 0.0, plus)).astype(BF16)
        own_ref[...] = total[2]

    tile = pl.BlockSpec((t, lanes), lambda i: (i, 0))
    three = pl.BlockSpec((3, t, lanes), lambda i: (0, i, 0))
    last = steps // 2 - 1
    return pl.pallas_call(
        kernel,
        grid=(steps,),
        in_specs=[
            three,
            three,
            pl.BlockSpec((1, t, lanes), lambda i: (dyh, jnp.minimum(i, last), 0)),
            pl.BlockSpec((1, t, lanes), lambda i: (dyh, jnp.maximum(i - last - 1, 0), 0)),
        ],
        out_specs=[tile] * 3,
        out_shape=[jax.ShapeDtypeStruct((tokens, lanes), d) for d in (BF16, BF16, F32)],
        compiler_params=pltpu.CompilerParams(vmem_limit_bytes=SMALL_LIMIT),
        cost_estimate=CHEAP,
        name=name,
    )(mine, back, via_minus, via_plus)


def body(carried_sum, x_panels, w_panels, cotangent):
    tokens, width = carried_sum.shape
    width_a = WIDTH_A
    rows = w_panels.shape[0]

    w_a, w_b = w_panels[:, :width_a], w_panels[:, width_a:]
    z_minus = shift(w_panels, "z", 1, NZ)
    z_plus = shift(w_panels, "z", -1, NZ)
    other_a = shift(w_a, "y_lo", 1, 2)
    pair = mark(flops(38 * 10**9), jnp.stack([x_panels, shift(x_panels, "y_hi", 1, 2)]))[0]
    x_minus = shift(pair, "x", 1, NX)
    x_plus = shift(pair, "x", -1, NX)
    z_minus, z_plus, other_a = mark(DEAR, z_minus, z_plus, other_a)
    up, down = z_minus[: rows // 2], z_plus[rows // 2 :]
    up, down, w_b, other_a, x_minus, x_plus = lax.optimization_barrier(
        (up, down, w_b, other_a, x_minus, x_plus)
    )
    far_top = shift(up, "z", 1, NZ)
    far_low = shift(down, "z", -1, NZ)
    other_b = shift(w_b, "y_lo", 1, 2)
    x_far = [shift(x_minus[0], "x", 1, NX), shift(x_plus[1], "x", -1, NX)]
    x_far = jnp.stack(x_far)
    near = jnp.concatenate([pair, x_plus, x_minus])
    far_a = jnp.concatenate([far_top[:, :width_a], far_low[:, :width_a]])
    far_b = jnp.concatenate([far_top[:, width_a:], far_low[:, width_a:]])
    send_a, near, x_far = lax.optimization_barrier(
        (other_a, near, x_far, far_top, far_low, other_b)
    )[:3]
    mine = [pair, x_plus, x_minus, x_far]
    theirs = [shift(near, "core", 1, 2), shift(x_far, "core", 1, 2)]
    other_minus_a = shift(send_a, "z", 1, NZ)
    other_plus_a = shift(send_a, "z", -1, NZ)
    other_far_a = shift(far_a, "y_lo", 1, 2)
    total, late_x = forward_early(
        ((0, 0), (0, 1), (0, 3), (1, 0)), ((0, 2), (1, 1), (1, 3), (1, 2)), mine, theirs, carried_sum,
        [(w_panels,), (z_plus,), (z_minus,), (other_a, other_b)],
    )
    send_b, send_far_b = lax.optimization_barrier(
        (other_b, far_b, other_minus_a, other_plus_a, other_far_a, total)
    )[:2]
    other_minus_b = shift(send_b, "z", 1, NZ)
    other_plus_b = shift(send_b, "z", -1, NZ)
    other_far_b = shift(send_far_b, "y_lo", 1, 2)
    done = forward_late(
        late_x, total, cotangent, [far_a, other_plus_a, other_minus_a, other_far_a], 0, [], "gelu_a"
    )
    activated, slope = forward_late(
        late_x, total, cotangent, [far_b, other_plus_b, other_minus_b, other_far_b], width_a, done, "gelu_b"
    )
    blocks = [(w_panels,), (z_plus,), (far_a, far_b), (z_minus,), (other_a, other_b)]
    blocks += [(other_plus_a, other_plus_b), (other_far_a, other_far_b), (other_minus_a, other_minus_b)]

    half = tokens // 2
    m, t = gradient(((2, 0), (2, 1)), slope, blocks, "grad_far")
    far_sum = (m.astype(F32) + shift(t, "core", 1, 2).astype(F32)).astype(BF16)
    up, down = lax.optimization_barrier((far_sum[:, :half], far_sum[:, half:]))
    via_minus = shift(up, "x", 1, NX)
    via_plus = shift(down, "x", -1, NX)

    slope = after(slope, up, down)
    m, t = gradient(((1, 1), (3, 1), (0, 1)), slope, blocks, "grad_1")
    via_minus, via_plus = mark(DEAR, via_minus, via_plus)
    up, down, own_1 = add_up(m, shift(t, "core", 1, 2), via_minus, via_plus, 1, "add_1")
    got_1 = shift(up, "x", 1, NX), shift(down, "x", -1, NX)

    slope = after(slope, up, down)
    m, t = gradient(((1, 0), (3, 0), (0, 0)), slope, blocks, "grad_0")
    got_1 = mark(DEAR, *got_1)
    m, via_minus, *got_1 = lax.optimization_barrier((m, via_minus, *got_1))
    up, down, own_0 = add_up(m, shift(t, "core", 1, 2), via_minus, via_plus, 0, "add_0")
    got_0 = shift(up, "x", 1, NX), shift(down, "x", -1, NX)
    to_other = own_1 + got_1[0].astype(F32) + got_1[1].astype(F32)
    from_other = shift(to_other.astype(BF16), "y_hi", 1, 2)
    input_grad = own_0 + got_0[0].astype(F32) + got_0[1].astype(F32) + from_other.astype(F32)
    return activated, input_grad.astype(BF16)


def solution(mesh):
    fine = Mesh(mesh.devices.reshape(2, 4, 4, 2, 2), ROWS_AXES + COLS_AXES)
    spec = P(ROWS_AXES, COLS_AXES)
    return jax.shard_map(
        body,
        mesh=fine,
        in_specs=(spec, spec, spec, spec),
        out_specs=(spec, spec),
        check_vma=False,
    )
```

```python
import jax
import jax.numpy as jnp
from jax import lax
from jax.experimental import pallas as pl
from jax.experimental.pallas import tpu as pltpu
from jax.sharding import Mesh, PartitionSpec as P

inv_root_two = 0.7071067811865476
inv_root_tau = 0.3989422804014327

NZ, NX = 4, 4
LANES = 256
WIDTH_A = 1280
ROWS_AXES = ("y_lo", "z")
COLS_AXES = ("x", "y_hi", "core")
F32, BF16 = jnp.float32, jnp.bfloat16
VMEM_LIMIT = 62 * 2**20
SMALL_LIMIT = 16 * 2**20
PARTS = 2
CHUNKS = 2


CHEAP = pl.CostEstimate(flops=1000, bytes_accessed=1000, transcendentals=0)


def flops(n):
    return pl.CostEstimate(flops=n, bytes_accessed=1000, transcendentals=0)


DEAR = flops(4 * 10**10)


def shift(value, axis, by, size):
    pairs = [(i, (i + by) % size) for i in range(size)]
    return lax.ppermute(value, axis, pairs)


def after(value, *deps):
    return lax.optimization_barrier((value, *deps))[0]


def panel_place(dy, dz):
    r = ((lax.axis_index("y_lo") + dy) & 1) * NZ + ((lax.axis_index("z") + dz) & (NZ - 1))
    dx = ((r >> 1) - lax.axis_index("x")) & (NX - 1)
    return (dx ^ (dx >> 1)) * 2 + ((r ^ lax.axis_index("y_hi")) & 1)


def block_place(dx, dyh):
    r = ((lax.axis_index("x") + dx) & (NX - 1)) * 2 + ((lax.axis_index("y_hi") + dyh) & 1)
    return (((r >> 2) ^ lax.axis_index("y_lo")) & 1) * NZ + ((r - lax.axis_index("z")) & (NZ - 1))


def forward_early(early, late, mine, theirs, start, shards):
    tokens, width = start.shape
    panels = sum(p.shape[0] for p in mine)
    n, n_p, n_late = len(shards), len(mine) + len(theirs), len(late)
    rows = shards[0][0].shape[0]
    pieces = [a for shard in shards for a in shard]

    def kernel(*refs):
        parts, (start_ref, *refs) = refs[:n_p], refs[n_p:]
        w_refs = refs[: len(pieces)]
        total_ref, late_x_ref, mine_ref, theirs_ref, sems, late_sems = refs[len(pieces) :]
        i = pl.program_id(0)
        own = lax.axis_index("core")
        out_copies = []
        for j, spot in enumerate(late):
            place = panel_place(*spot)
            for k, buf in enumerate((mine_ref, theirs_ref)):
                column = pl.multiple_of((2 * j + jnp.where(own == k, 0, 1)) * LANES, LANES)
                out_copies.append(
                    pltpu.make_async_copy(
                        buf.at[place],
                        late_x_ref.at[:, pl.ds(column, LANES)],
                        late_sems.at[2 * j + k],
                    )
                )

        @pl.when(i == 0)
        def _():
            copies = []
            for buf, own_parts in ((mine_ref, parts[: len(mine)]), (theirs_ref, parts[len(mine) :])):
                to = 0
                for part in own_parts:
                    held = buf.at[pl.ds(to, part.shape[0])]
                    copies.append(pltpu.make_async_copy(part, held, sems.at[len(copies)]))
                    to += part.shape[0]
            for c in copies:
                c.start()
            for c in copies:
                c.wait()
            for c in out_copies:
                c.start()

        lo = pl.multiple_of(own * LANES, LANES)
        hi = pl.multiple_of((1 - own) * LANES, LANES)
        lhs = jnp.concatenate(
            [r[panel_place(*spot)] for spot in early for r in (mine_ref, theirs_ref)], axis=1
        )
        rhs, at = [], 0
        for shard in shards:
            held = w_refs[at : at + len(shard)]
            for o in (lo, hi):
                block = held[0][pl.ds(o, LANES), :]
                if len(shard) == 2:
                    edge = shard[0].shape[1] // LANES
                    block = jnp.where(i < edge, block, held[1][pl.ds(o, LANES), :])
                rhs.append(block)
            at += len(shard)
        rhs = jnp.concatenate(rhs, axis=0)
        total_ref[...] = start_ref[...] + jnp.dot(lhs, rhs, preferred_element_type=F32)

        @pl.when(i == pl.num_programs(0) - 1)
        def _():
            for c in out_copies:
                c.wait()

    def piece_specs(shard):
        if len(shard) == 1:
            return [pl.BlockSpec((rows, LANES), lambda i, *_: (0, i))]
        edge = shard[0].shape[1] // LANES
        return [
            pl.BlockSpec((rows, LANES), lambda i, *_: (0, jnp.minimum(i, edge - 1))),
            pl.BlockSpec((rows, LANES), lambda i, *_: (0, jnp.maximum(i - edge, 0))),
        ]

    tile = pl.BlockSpec((tokens, LANES), lambda i, *_: (0, i))
    hbm = pl.BlockSpec(memory_space=pl.ANY)
    return pl.pallas_call(
        kernel,
        grid=(width // LANES,),
        in_specs=[hbm] * n_p + [tile] + [p for shard in shards for p in piece_specs(shard)],
        out_specs=[tile, hbm],
        scratch_shapes=[pltpu.VMEM((panels, tokens, LANES), BF16)] * 2
        + [pltpu.SemaphoreType.DMA((n_p,)), pltpu.SemaphoreType.DMA((2 * n_late,))],
        out_shape=[
            jax.ShapeDtypeStruct((tokens, width), F32),
            jax.ShapeDtypeStruct((tokens, 2 * n_late * LANES), BF16),
        ],
        compiler_params=pltpu.CompilerParams(vmem_limit_bytes=VMEM_LIMIT),
        cost_estimate=CHEAP,
        name="early",
    )(*mine, *theirs, start, *pieces)


def gelu(preact, cotangent):
    normal_cdf = 0.5 * (1.0 + lax.erf(preact * inv_root_two))
    normal_pdf = jnp.exp(-0.5 * preact * preact) * inv_root_tau
    slope = cotangent.astype(F32) * (normal_cdf + preact * normal_pdf)
    return (preact * normal_cdf).astype(BF16), slope.astype(BF16)


def forward_late(late_x, total, cotangent, shards, name):
    tokens, width = total.shape
    rows, cols = shards[0].shape
    n = len(shards)
    depth = late_x.shape[1]
    t = tokens // PARTS

    def kernel(x_ref, start_ref, cot_ref, *refs):
        w_refs, (act_ref, slope_ref) = refs[:n], refs[-2:]
        rhs = jnp.concatenate([w[...] for w in w_refs], axis=0)
        for p in range(PARTS):
            at = pl.ds(p * t, t)
            preact = start_ref[at, :] + jnp.dot(x_ref[at, :], rhs, preferred_element_type=F32)
            act_ref[at, :], slope_ref[at, :] = gelu(preact, cot_ref[at, :])

    tile = pl.BlockSpec((tokens, LANES), lambda i: (0, i))
    return pl.pallas_call(
        kernel,
        grid=(cols // LANES,),
        in_specs=[pl.BlockSpec((tokens, depth), lambda i: (0, 0)), tile, tile]
        + [pl.BlockSpec((rows, LANES), lambda i: (0, i))] * n,
        out_specs=[tile, tile],
        out_shape=[jax.ShapeDtypeStruct((tokens, width), BF16)] * 2,
        compiler_params=pltpu.CompilerParams(vmem_limit_bytes=VMEM_LIMIT),
        cost_estimate=CHEAP,
        name=name,
    )(late_x, total, cotangent, *shards)


def gradient(places, slope, blocks, name, last=None):
    tokens, width = slope.shape
    n_last = 0
    if last is not None:
        late_x, total, cotangent, shards, activated = last
        cols = shards[0].shape[1]
        edge = width - cols
        depth = late_x.shape[1]
        last_args = [late_x, total, cotangent, *shards, activated]
        n_last = len(last_args)
    rows = 2 * LANES
    n = len(places)
    arrays = [a for shard in blocks for a in shard]
    t = tokens // CHUNKS

    def kernel(s_hbm, *refs):
        last_refs, refs = refs[:n_last], refs[n_last:]
        a_refs, refs = refs[: len(arrays)], refs[len(arrays) :]
        mine_hbm, theirs_hbm, *refs = refs
        if last is not None:
            s_out, act_out, *refs = refs
            x_buf, total_buf, cot_buf, shard_buf, act_buf, *refs, l_sem, x_sem, act_sem = refs
        s_buf, w_buf, out_buf, s_sem, w_sem, out_sem = refs

        def fetch(k):
            wanted = block_place(*places[k])
            at = 0
            for j, shard in enumerate(blocks):
                held = a_refs[at : at + len(shard)]
                at += len(shard)

                @pl.when(wanted == j)
                def _():
                    to = 0
                    for ref in held:
                        w = ref.shape[1]
                        pltpu.make_async_copy(ref, w_buf.at[k, :, pl.ds(to, w)], w_sem.at[k]).start()
                        to += w

        chunks = [pl.ds(c * t, t) for c in range(CHUNKS)]
        had = width if last is None else edge
        loads = [
            pltpu.make_async_copy(
                s_hbm.at[at, pl.ds(0, had)], s_buf.at[at, pl.ds(0, had)], s_sem.at[c]
            )
            for c, at in enumerate(chunks)
        ]
        stores = []
        if last is None:
            fetch(0)
            for load in loads:
                load.start()
        else:
            x_hbm, total_hbm, cot_hbm, *shard_hbm = last_refs[:-1]
            tail = pl.ds(edge, cols)
            first = [
                pltpu.make_async_copy(ref, shard_buf.at[pl.ds(j * rows, rows)], l_sem.at[j])
                for j, ref in enumerate(shard_hbm)
            ]
            by_chunk = [
                [
                    pltpu.make_async_copy(x_hbm.at[at], x_buf.at[at], x_sem.at[0, c]),
                    pltpu.make_async_copy(total_hbm.at[at, tail], total_buf.at[at], x_sem.at[1, c]),
                    pltpu.make_async_copy(cot_hbm.at[at, tail], cot_buf.at[at], x_sem.at[2, c]),
                ]
                for c, at in enumerate(chunks)
            ]
            for load in first + sum(by_chunk, []):
                load.start()
            for load in loads:
                load.start()
            fetch(0)
            for load in first:
                load.wait()
            for c, at in enumerate(chunks):
                for load in by_chunk[c]:
                    load.wait()
                for b in range(cols // LANES):
                    here = pl.ds(b * LANES, LANES)
                    preact = total_buf[at, here] + jnp.dot(
                        x_buf[at, :], shard_buf[:, here], preferred_element_type=F32
                    )
                    act_buf[at, here], s_buf[at, pl.ds(edge + b * LANES, LANES)] = gelu(
                        preact, cot_buf[at, here]
                    )
                stores.append(pltpu.make_async_copy(act_buf.at[at], act_out.at[at, tail], act_sem.at[0, c]))
                stores.append(
                    pltpu.make_async_copy(s_buf.at[at, tail], s_out.at[at, tail], act_sem.at[1, c])
                )
                stores[-2].start()
                stores[-1].start()
        own = lax.axis_index("core")
        for k in range(n):
            if k + 1 < n:
                fetch(k + 1)
            pltpu.make_async_copy(a_refs[0], w_buf.at[k], w_sem.at[k]).wait()
            for c, at in enumerate(chunks):
                if k == 0:
                    loads[c].wait()
                for h, (half, out) in enumerate(((1 - own, theirs_hbm), (own, mine_hbm))):
                    part = w_buf[k, pl.ds(pl.multiple_of(half * LANES, LANES), LANES), :]
                    out_buf[k, h, at, :] = lax.dot_general(
                        s_buf[at, :], part, (((1,), (1,)), ((), ())), preferred_element_type=F32
                    ).astype(BF16)
                    store = pltpu.make_async_copy(
                        out_buf.at[k, h, at], out.at[k, at], out_sem.at[k, h, c]
                    )
                    store.start()
                    stores.append(store)
        for store in stores:
            store.wait()

    last_scratch, last_sems, last_out, aliases = [], [], [], {}
    if last is not None:
        last_scratch = [
            pltpu.VMEM((tokens, depth), BF16),
            pltpu.VMEM((tokens, cols), F32),
            pltpu.VMEM((tokens, cols), BF16),
            pltpu.VMEM((depth, cols), BF16),
            pltpu.VMEM((tokens, cols), BF16),
        ]
        last_sems = [
            pltpu.SemaphoreType.DMA((len(shards),)),
            pltpu.SemaphoreType.DMA((3, CHUNKS)),
            pltpu.SemaphoreType.DMA((2, CHUNKS)),
        ]
        last_out = [jax.ShapeDtypeStruct((tokens, width), BF16)] * 2
        aliases = {0: 2, n_last: 3}
    hbm = pl.BlockSpec(memory_space=pl.ANY)
    return pl.pallas_call(
        kernel,
        in_specs=[hbm] * (1 + n_last + len(arrays)),
        out_specs=[hbm] * (2 + len(last_out)),
        scratch_shapes=last_scratch
        + [
            pltpu.VMEM((tokens, width), BF16),
            pltpu.VMEM((n, rows, width), BF16),
            pltpu.VMEM((n, 2, tokens, LANES), BF16),
            pltpu.SemaphoreType.DMA((CHUNKS,)),
            pltpu.SemaphoreType.DMA((n,)),
            pltpu.SemaphoreType.DMA((n, 2, CHUNKS)),
        ]
        + last_sems,
        out_shape=[jax.ShapeDtypeStruct((n, tokens, LANES), BF16)] * 2 + last_out,
        input_output_aliases=aliases,
        compiler_params=pltpu.CompilerParams(vmem_limit_bytes=VMEM_LIMIT),
        cost_estimate=CHEAP,
        name=name,
    )(slope, *(last_args if last is not None else []), *arrays)


def mark(cost, *arrays):
    n = len(arrays)
    any_space = [pl.BlockSpec(memory_space=pl.ANY)] * n
    return pl.pallas_call(
        lambda *refs: None,
        in_specs=any_space,
        out_specs=any_space,
        out_shape=[jax.ShapeDtypeStruct(a.shape, a.dtype) for a in arrays],
        input_output_aliases={i: i for i in range(n)},
        compiler_params=pltpu.CompilerParams(vmem_limit_bytes=SMALL_LIMIT),
        cost_estimate=cost,
        name="mark",
    )(*arrays)


def add_up(mine, back, via_minus, via_plus, dyh, got, name):
    tokens, lanes = mine.shape[1:]
    steps = 2
    t = tokens // steps

    def kernel(mine_ref, back_ref, minus_ref, plus_ref, *refs):
        got_refs, (up_ref, down_ref, *own_ref) = refs[: len(got)], refs[len(got) :]
        first = pl.program_id(0) < steps // 2
        total = mine_ref[...].astype(F32) + back_ref[...].astype(F32)
        minus, plus = minus_ref[0].astype(F32), plus_ref[0].astype(F32)
        up_ref[...] = (total[0] + jnp.where(first, minus, 0.0)).astype(BF16)
        down_ref[...] = (total[1] + jnp.where(first, 0.0, plus)).astype(BF16)
        if got:
            own = total[2]
            for ref in got_refs:
                own = own + ref[...].astype(F32)
            own_ref[0][...] = own.astype(BF16)

    tile = pl.BlockSpec((t, lanes), lambda i: (i, 0))
    stack = pl.BlockSpec((mine.shape[0], t, lanes), lambda i: (0, i, 0))
    last = steps // 2 - 1
    n_out = 3 if got else 2
    return pl.pallas_call(
        kernel,
        grid=(steps,),
        in_specs=[
            stack,
            stack,
            pl.BlockSpec((1, t, lanes), lambda i: (dyh, jnp.minimum(i, last), 0)),
            pl.BlockSpec((1, t, lanes), lambda i: (dyh, jnp.maximum(i - last - 1, 0), 0)),
        ]
        + [tile] * len(got),
        out_specs=[tile] * n_out,
        out_shape=[jax.ShapeDtypeStruct((tokens, lanes), BF16)] * n_out,
        compiler_params=pltpu.CompilerParams(vmem_limit_bytes=SMALL_LIMIT),
        cost_estimate=CHEAP,
        name=name,
    )(mine, back, via_minus, via_plus, *got)


def body(carried_sum, x_panels, w_panels, cotangent):
    tokens, width = carried_sum.shape
    width_a = WIDTH_A
    rows = w_panels.shape[0]

    w_a, w_b = w_panels[:, :width_a], w_panels[:, width_a:]
    z_minus = shift(w_panels, "z", 1, NZ)
    z_plus = shift(w_panels, "z", -1, NZ)
    other_a = shift(w_a, "y_lo", 1, 2)
    pair = mark(flops(38 * 10**9), jnp.stack([x_panels, shift(x_panels, "y_hi", 1, 2)]))[0]
    x_minus = shift(pair, "x", 1, NX)
    x_plus = shift(pair, "x", -1, NX)
    z_minus, z_plus = mark(flops(80 * 10**9), z_minus, z_plus)
    other_a = mark(DEAR, other_a)[0]
    up, down = z_minus[: rows // 2], z_plus[rows // 2 :]
    up, down, w_b, other_a, x_minus, x_plus = lax.optimization_barrier(
        (up, down, w_b, other_a, x_minus, x_plus)
    )
    far_top = shift(up, "z", 1, NZ)
    far_low = shift(down, "z", -1, NZ)
    other_b = shift(w_b, "y_lo", 1, 2)
    x_far = [shift(x_minus[0], "x", 1, NX), shift(x_plus[1], "x", -1, NX)]
    x_far = jnp.stack(x_far)
    near = jnp.concatenate([pair, x_plus, x_minus])
    far_a = jnp.concatenate([far_top[:, :width_a], far_low[:, :width_a]])
    far_b = jnp.concatenate([far_top[:, width_a:], far_low[:, width_a:]])
    send_a, near, x_far = lax.optimization_barrier(
        (other_a, near, x_far, far_top, far_low, other_b)
    )[:3]
    mine = [pair, x_plus, x_minus, x_far]
    theirs = [shift(near, "core", 1, 2), shift(x_far, "core", 1, 2)]
    other_minus_a = shift(send_a, "z", 1, NZ)
    other_plus_a = shift(send_a, "z", -1, NZ)
    other_far_a = shift(far_a, "y_lo", 1, 2)
    total, late_x = forward_early(
        ((0, 0), (0, 1), (0, 3), (1, 0), (0, 2)), ((1, 1), (1, 3), (1, 2)), mine, theirs, carried_sum,
        [(w_panels,), (z_plus,), (z_minus,), (other_a, other_b), (far_a, far_b)],
    )
    send_b, send_far_b = lax.optimization_barrier(
        (other_b, far_b, other_minus_a, other_plus_a, other_far_a, total)
    )[:2]
    other_minus_b = shift(send_b, "z", 1, NZ)
    other_plus_b = shift(send_b, "z", -1, NZ)
    other_far_b = shift(send_far_b, "y_lo", 1, 2)
    activated, slope = forward_late(
        late_x, total, cotangent, [other_plus_a, other_minus_a, other_far_a], "gelu_a"
    )
    last = (late_x, total, cotangent, [other_plus_b, other_minus_b, other_far_b], activated)
    blocks = [(w_panels,), (z_plus,), (far_a, far_b), (z_minus,), (other_a, other_b)]
    blocks += [(other_plus_a, other_plus_b), (other_far_a, other_far_b), (other_minus_a, other_minus_b)]

    half = tokens // 2
    m, t, slope, activated = gradient(((2, 0), (2, 1)), slope, blocks, "grad_far", last)
    far_sum = (m.astype(F32) + shift(t, "core", 1, 2).astype(F32)).astype(BF16)
    up, down = lax.optimization_barrier((far_sum[:, :half], far_sum[:, half:]))
    via_minus = shift(up, "x", 1, NX)
    via_plus = shift(down, "x", -1, NX)

    slope = after(slope, up, down)
    m, t = gradient(((1, 1), (3, 1)), slope, blocks, "grad_1")
    via_minus, via_plus = mark(DEAR, via_minus, via_plus)
    up, down = add_up(m, shift(t, "core", 1, 2), via_minus, via_plus, 1, [], "add_1")
    got_1 = shift(up, "x", 1, NX), shift(down, "x", -1, NX)

    slope = after(slope, up, down)
    m, t = gradient(((1, 0), (3, 0), (0, 1)), slope, blocks, "grad_0")
    got_1 = mark(DEAR, *got_1)
    up, down, to_other = add_up(m, shift(t, "core", 1, 2), via_minus, via_plus, 0, got_1, "add_0")
    got_0 = shift(up, "x", 1, NX), shift(down, "x", -1, NX)
    from_other = shift(to_other, "y_hi", 1, 2)

    slope = after(slope, up, down, to_other)
    m, t = gradient(((0, 0),), slope, blocks, "grad_own")
    got_0 = mark(DEAR, *got_0)
    from_other = mark(flops(60 * 10**9), from_other)[0]
    input_grad = m[0].astype(F32) + shift(t, "core", 1, 2)[0].astype(F32)
    for part in (*got_0, from_other):
        input_grad = input_grad + part.astype(F32)
    input_grad = input_grad.astype(BF16)
    return activated, input_grad.astype(BF16)


def solution(mesh):
    fine = Mesh(mesh.devices.reshape(2, 4, 4, 2, 2), ROWS_AXES + COLS_AXES)
    spec = P(ROWS_AXES, COLS_AXES)
    return jax.shard_map(
        body,
        mesh=fine,
        in_specs=(spec, spec, spec, spec),
        out_specs=(spec, spec),
        check_vma=False,
    )
```

```python
import jax
import jax.numpy as jnp
from jax import lax
from jax.experimental import pallas as pl
from jax.experimental.pallas import tpu as pltpu
from jax.sharding import Mesh, PartitionSpec as P

inv_root_two = 0.7071067811865476
inv_root_tau = 0.3989422804014327

NZ, NX = 4, 4
LANES = 256
WIDTH_A = 1280
ROWS_AXES = ("y_lo", "z")
COLS_AXES = ("x", "y_hi", "core")
F32, BF16 = jnp.float32, jnp.bfloat16
VMEM_LIMIT = 62 * 2**20
SMALL_LIMIT = 16 * 2**20
PARTS = 2
CHUNKS = 2


CHEAP = pl.CostEstimate(flops=1000, bytes_accessed=1000, transcendentals=0)


def flops(n):
    return pl.CostEstimate(flops=n, bytes_accessed=1000, transcendentals=0)


DEAR = flops(4 * 10**10)
SOME = flops(2 * 10**10)


def shift(value, axis, by, size):
    pairs = [(i, (i + by) % size) for i in range(size)]
    return lax.ppermute(value, axis, pairs)


def after(value, *deps):
    return lax.optimization_barrier((value, *deps))[0]


def panel_place(dy, dz):
    r = ((lax.axis_index("y_lo") + dy) & 1) * NZ + ((lax.axis_index("z") + dz) & (NZ - 1))
    dx = ((r >> 1) - lax.axis_index("x")) & (NX - 1)
    return (dx ^ (dx >> 1)) * 2 + ((r ^ lax.axis_index("y_hi")) & 1)


def block_place(dx, dyh):
    r = ((lax.axis_index("x") + dx) & (NX - 1)) * 2 + ((lax.axis_index("y_hi") + dyh) & 1)
    return (((r >> 2) ^ lax.axis_index("y_lo")) & 1) * NZ + ((r - lax.axis_index("z")) & (NZ - 1))


def forward_early(early, late, mine, theirs, start, shards):
    tokens, width = start.shape
    panels = sum(p.shape[0] for p in mine)
    n, n_p, n_late = len(shards), len(mine) + len(theirs), len(late)
    rows = shards[0][0].shape[0]
    pieces = [a for shard in shards for a in shard]

    def kernel(*refs):
        parts, (start_ref, *refs) = refs[:n_p], refs[n_p:]
        w_refs = refs[: len(pieces)]
        total_ref, late_x_ref, mine_ref, theirs_ref, sems, late_sems = refs[len(pieces) :]
        i = pl.program_id(0)
        own = lax.axis_index("core")
        out_copies = []
        for j, spot in enumerate(late):
            place = panel_place(*spot)
            for k, buf in enumerate((mine_ref, theirs_ref)):
                column = pl.multiple_of((2 * j + jnp.where(own == k, 0, 1)) * LANES, LANES)
                out_copies.append(
                    pltpu.make_async_copy(
                        buf.at[place],
                        late_x_ref.at[:, pl.ds(column, LANES)],
                        late_sems.at[2 * j + k],
                    )
                )

        @pl.when(i == 0)
        def _():
            copies = []
            for buf, own_parts in ((mine_ref, parts[: len(mine)]), (theirs_ref, parts[len(mine) :])):
                to = 0
                for part in own_parts:
                    held = buf.at[pl.ds(to, part.shape[0])]
                    copies.append(pltpu.make_async_copy(part, held, sems.at[len(copies)]))
                    to += part.shape[0]
            for c in copies:
                c.start()
            for c in copies:
                c.wait()
            for c in out_copies:
                c.start()

        lo = pl.multiple_of(own * LANES, LANES)
        hi = pl.multiple_of((1 - own) * LANES, LANES)
        lhs = jnp.concatenate(
            [r[panel_place(*spot)] for spot in early for r in (mine_ref, theirs_ref)], axis=1
        )
        rhs, at = [], 0
        for shard in shards:
            held = w_refs[at : at + len(shard)]
            for o in (lo, hi):
                block = held[0][pl.ds(o, LANES), :]
                if len(shard) == 2:
                    edge = shard[0].shape[1] // LANES
                    block = jnp.where(i < edge, block, held[1][pl.ds(o, LANES), :])
                rhs.append(block)
            at += len(shard)
        rhs = jnp.concatenate(rhs, axis=0)
        total_ref[...] = start_ref[...] + jnp.dot(lhs, rhs, preferred_element_type=F32)

        @pl.when(i == pl.num_programs(0) - 1)
        def _():
            for c in out_copies:
                c.wait()

    def piece_specs(shard):
        if len(shard) == 1:
            return [pl.BlockSpec((rows, LANES), lambda i, *_: (0, i))]
        edge = shard[0].shape[1] // LANES
        return [
            pl.BlockSpec((rows, LANES), lambda i, *_: (0, jnp.minimum(i, edge - 1))),
            pl.BlockSpec((rows, LANES), lambda i, *_: (0, jnp.maximum(i - edge, 0))),
        ]

    tile = pl.BlockSpec((tokens, LANES), lambda i, *_: (0, i))
    hbm = pl.BlockSpec(memory_space=pl.ANY)
    return pl.pallas_call(
        kernel,
        grid=(width // LANES,),
        in_specs=[hbm] * n_p + [tile] + [p for shard in shards for p in piece_specs(shard)],
        out_specs=[tile, hbm],
        scratch_shapes=[pltpu.VMEM((panels, tokens, LANES), BF16)] * 2
        + [pltpu.SemaphoreType.DMA((n_p,)), pltpu.SemaphoreType.DMA((2 * n_late,))],
        out_shape=[
            jax.ShapeDtypeStruct((tokens, width), F32),
            jax.ShapeDtypeStruct((tokens, 2 * n_late * LANES), BF16),
        ],
        compiler_params=pltpu.CompilerParams(vmem_limit_bytes=VMEM_LIMIT),
        cost_estimate=CHEAP,
        name="early",
    )(*mine, *theirs, start, *pieces)


def gelu(preact, cotangent):
    normal_cdf = 0.5 * (1.0 + lax.erf(preact * inv_root_two))
    normal_pdf = jnp.exp(-0.5 * preact * preact) * inv_root_tau
    slope = cotangent.astype(F32) * (normal_cdf + preact * normal_pdf)
    return (preact * normal_cdf).astype(BF16), slope.astype(BF16)


def forward_late(late_x, total, cotangent, shards, name):
    tokens, width = total.shape
    rows, cols = shards[0].shape
    n = len(shards)
    depth = late_x.shape[1]
    t = tokens // PARTS

    def kernel(x_ref, start_ref, cot_ref, *refs):
        w_refs, (act_ref, slope_ref) = refs[:n], refs[-2:]
        rhs = jnp.concatenate([w[...] for w in w_refs], axis=0)
        for p in range(PARTS):
            at = pl.ds(p * t, t)
            preact = start_ref[at, :] + jnp.dot(x_ref[at, :], rhs, preferred_element_type=F32)
            act_ref[at, :], slope_ref[at, :] = gelu(preact, cot_ref[at, :])

    tile = pl.BlockSpec((tokens, LANES), lambda i: (0, i))
    return pl.pallas_call(
        kernel,
        grid=(cols // LANES,),
        in_specs=[pl.BlockSpec((tokens, depth), lambda i: (0, 0)), tile, tile]
        + [pl.BlockSpec((rows, LANES), lambda i: (0, i))] * n,
        out_specs=[tile, tile],
        out_shape=[jax.ShapeDtypeStruct((tokens, width), BF16)] * 2,
        compiler_params=pltpu.CompilerParams(vmem_limit_bytes=VMEM_LIMIT),
        cost_estimate=CHEAP,
        name=name,
    )(late_x, total, cotangent, *shards)


def gradient(places, slope, blocks, name, last=None):
    tokens, width = slope.shape
    n_last = 0
    if last is not None:
        late_x, total, cotangent, shards, activated = last
        cols = shards[0].shape[1]
        edge = width - cols
        depth = late_x.shape[1]
        last_args = [late_x, total, cotangent, *shards, activated]
        n_last = len(last_args)
    rows = 2 * LANES
    n = len(places)
    arrays = [a for shard in blocks for a in shard]
    t = tokens // CHUNKS

    def kernel(s_hbm, *refs):
        last_refs, refs = refs[:n_last], refs[n_last:]
        a_refs, refs = refs[: len(arrays)], refs[len(arrays) :]
        mine_hbm, theirs_hbm, *refs = refs
        if last is not None:
            s_out, act_out, *refs = refs
            x_buf, total_buf, cot_buf, shard_buf, act_buf, *refs, l_sem, x_sem, act_sem = refs
        s_buf, w_buf, out_buf, s_sem, w_sem, out_sem = refs

        def fetch(k):
            wanted = block_place(*places[k])
            at = 0
            for j, shard in enumerate(blocks):
                held = a_refs[at : at + len(shard)]
                at += len(shard)

                @pl.when(wanted == j)
                def _():
                    to = 0
                    for ref in held:
                        w = ref.shape[1]
                        pltpu.make_async_copy(ref, w_buf.at[k, :, pl.ds(to, w)], w_sem.at[k]).start()
                        to += w

        chunks = [pl.ds(c * t, t) for c in range(CHUNKS)]
        had = width if last is None else edge
        loads = [
            pltpu.make_async_copy(
                s_hbm.at[at, pl.ds(0, had)], s_buf.at[at, pl.ds(0, had)], s_sem.at[c]
            )
            for c, at in enumerate(chunks)
        ]
        stores = []
        if last is None:
            fetch(0)
            for load in loads:
                load.start()
        else:
            x_hbm, total_hbm, cot_hbm, *shard_hbm = last_refs[:-1]
            tail = pl.ds(edge, cols)
            first = [
                pltpu.make_async_copy(ref, shard_buf.at[pl.ds(j * rows, rows)], l_sem.at[j])
                for j, ref in enumerate(shard_hbm)
            ]
            by_chunk = [
                [
                    pltpu.make_async_copy(x_hbm.at[at], x_buf.at[at], x_sem.at[0, c]),
                    pltpu.make_async_copy(total_hbm.at[at, tail], total_buf.at[at], x_sem.at[1, c]),
                    pltpu.make_async_copy(cot_hbm.at[at, tail], cot_buf.at[at], x_sem.at[2, c]),
                ]
                for c, at in enumerate(chunks)
            ]
            for load in first + sum(by_chunk, []):
                load.start()
            for load in loads:
                load.start()
            fetch(0)
            for load in first:
                load.wait()
            for c, at in enumerate(chunks):
                for load in by_chunk[c]:
                    load.wait()
                for b in range(cols // LANES):
                    here = pl.ds(b * LANES, LANES)
                    preact = total_buf[at, here] + jnp.dot(
                        x_buf[at, :], shard_buf[:, here], preferred_element_type=F32
                    )
                    act_buf[at, here], s_buf[at, pl.ds(edge + b * LANES, LANES)] = gelu(
                        preact, cot_buf[at, here]
                    )
                stores.append(pltpu.make_async_copy(act_buf.at[at], act_out.at[at, tail], act_sem.at[0, c]))
                stores.append(
                    pltpu.make_async_copy(s_buf.at[at, tail], s_out.at[at, tail], act_sem.at[1, c])
                )
                stores[-2].start()
                stores[-1].start()
        own = lax.axis_index("core")
        for k in range(n):
            if k + 1 < n:
                fetch(k + 1)
            pltpu.make_async_copy(a_refs[0], w_buf.at[k], w_sem.at[k]).wait()
            for c, at in enumerate(chunks):
                if k == 0:
                    loads[c].wait()
                for h, (half, out) in enumerate(((1 - own, theirs_hbm), (own, mine_hbm))):
                    part = w_buf[k, pl.ds(pl.multiple_of(half * LANES, LANES), LANES), :]
                    out_buf[k, h, at, :] = lax.dot_general(
                        s_buf[at, :], part, (((1,), (1,)), ((), ())), preferred_element_type=F32
                    ).astype(BF16)
                    store = pltpu.make_async_copy(
                        out_buf.at[k, h, at], out.at[k, at], out_sem.at[k, h, c]
                    )
                    store.start()
                    stores.append(store)
        for store in stores:
            store.wait()

    last_scratch, last_sems, last_out, aliases = [], [], [], {}
    if last is not None:
        last_scratch = [
            pltpu.VMEM((tokens, depth), BF16),
            pltpu.VMEM((tokens, cols), F32),
            pltpu.VMEM((tokens, cols), BF16),
            pltpu.VMEM((depth, cols), BF16),
            pltpu.VMEM((tokens, cols), BF16),
        ]
        last_sems = [
            pltpu.SemaphoreType.DMA((len(shards),)),
            pltpu.SemaphoreType.DMA((3, CHUNKS)),
            pltpu.SemaphoreType.DMA((2, CHUNKS)),
        ]
        last_out = [jax.ShapeDtypeStruct((tokens, width), BF16)] * 2
        aliases = {0: 2, n_last: 3}
    hbm = pl.BlockSpec(memory_space=pl.ANY)
    return pl.pallas_call(
        kernel,
        in_specs=[hbm] * (1 + n_last + len(arrays)),
        out_specs=[hbm] * (2 + len(last_out)),
        scratch_shapes=last_scratch
        + [
            pltpu.VMEM((tokens, width), BF16),
            pltpu.VMEM((n, rows, width), BF16),
            pltpu.VMEM((n, 2, tokens, LANES), BF16),
            pltpu.SemaphoreType.DMA((CHUNKS,)),
            pltpu.SemaphoreType.DMA((n,)),
            pltpu.SemaphoreType.DMA((n, 2, CHUNKS)),
        ]
        + last_sems,
        out_shape=[jax.ShapeDtypeStruct((n, tokens, LANES), BF16)] * 2 + last_out,
        input_output_aliases=aliases,
        compiler_params=pltpu.CompilerParams(vmem_limit_bytes=VMEM_LIMIT),
        cost_estimate=CHEAP,
        name=name,
    )(slope, *(last_args if last is not None else []), *arrays)


def mark(cost, *arrays, limit=SMALL_LIMIT):
    n = len(arrays)
    any_space = [pl.BlockSpec(memory_space=pl.ANY)] * n
    return pl.pallas_call(
        lambda *refs: None,
        in_specs=any_space,
        out_specs=any_space,
        out_shape=[jax.ShapeDtypeStruct(a.shape, a.dtype) for a in arrays],
        input_output_aliases={i: i for i in range(n)},
        compiler_params=pltpu.CompilerParams(vmem_limit_bytes=limit),
        cost_estimate=cost,
        name="mark",
    )(*arrays)


def add_up(mine, back, via_minus, via_plus, dyh, got, name):
    tokens, lanes = mine.shape[1:]
    steps = 2
    t = tokens // steps

    def kernel(mine_ref, back_ref, minus_ref, plus_ref, *refs):
        got_refs, (up_ref, down_ref, *own_ref) = refs[: len(got)], refs[len(got) :]
        first = pl.program_id(0) < steps // 2
        total = mine_ref[...].astype(F32) + back_ref[...].astype(F32)
        minus, plus = minus_ref[0].astype(F32), plus_ref[0].astype(F32)
        up_ref[...] = (total[0] + jnp.where(first, minus, 0.0)).astype(BF16)
        down_ref[...] = (total[1] + jnp.where(first, 0.0, plus)).astype(BF16)
        if got:
            own = total[2]
            for ref in got_refs:
                own = own + ref[...].astype(F32)
            own_ref[0][...] = own.astype(BF16)

    tile = pl.BlockSpec((t, lanes), lambda i: (i, 0))
    stack = pl.BlockSpec((mine.shape[0], t, lanes), lambda i: (0, i, 0))
    last = steps // 2 - 1
    n_out = 3 if got else 2
    return pl.pallas_call(
        kernel,
        grid=(steps,),
        in_specs=[
            stack,
            stack,
            pl.BlockSpec((1, t, lanes), lambda i: (dyh, jnp.minimum(i, last), 0)),
            pl.BlockSpec((1, t, lanes), lambda i: (dyh, jnp.maximum(i - last - 1, 0), 0)),
        ]
        + [tile] * len(got),
        out_specs=[tile] * n_out,
        out_shape=[jax.ShapeDtypeStruct((tokens, lanes), BF16)] * n_out,
        compiler_params=pltpu.CompilerParams(vmem_limit_bytes=SMALL_LIMIT),
        cost_estimate=CHEAP,
        name=name,
    )(mine, back, via_minus, via_plus, *got)


def body(carried_sum, x_panels, w_panels, cotangent):
    tokens, width = carried_sum.shape
    width_a = WIDTH_A
    rows = w_panels.shape[0]

    w_a, w_b = w_panels[:, :width_a], w_panels[:, width_a:]
    z_minus = shift(w_panels, "z", 1, NZ)
    z_plus = shift(w_panels, "z", -1, NZ)
    other_a = shift(w_a, "y_lo", 1, 2)
    pair = mark(flops(38 * 10**9), jnp.stack([x_panels, shift(x_panels, "y_hi", 1, 2)]))[0]
    x_minus = shift(pair, "x", 1, NX)
    x_plus = shift(pair, "x", -1, NX)
    z_minus, z_plus = mark(flops(80 * 10**9), z_minus, z_plus)
    other_a = mark(DEAR, other_a)[0]
    up, down = z_minus[: rows // 2], z_plus[rows // 2 :]
    up, down, w_b, other_a, x_minus, x_plus = lax.optimization_barrier(
        (up, down, w_b, other_a, x_minus, x_plus)
    )
    far_top = shift(up, "z", 1, NZ)
    far_low = shift(down, "z", -1, NZ)
    other_b = shift(w_b, "y_lo", 1, 2)
    x_far = [shift(x_minus[0], "x", 1, NX), shift(x_plus[1], "x", -1, NX)]
    x_far = jnp.stack(x_far)
    near = jnp.concatenate([pair, x_plus, x_minus])
    far_a = jnp.concatenate([far_top[:, :width_a], far_low[:, :width_a]])
    far_b = jnp.concatenate([far_top[:, width_a:], far_low[:, width_a:]])
    send_a, near, x_far = lax.optimization_barrier(
        (other_a, near, x_far, far_top, far_low, other_b)
    )[:3]
    mine = [pair, x_plus, x_minus, x_far]
    theirs = [shift(near, "core", 1, 2), shift(x_far, "core", 1, 2)]
    other_minus_a = shift(send_a, "z", 1, NZ)
    other_plus_a = shift(send_a, "z", -1, NZ)
    other_far_a = shift(far_a, "y_lo", 1, 2)
    total, late_x = forward_early(
        ((0, 0), (0, 1), (0, 3), (1, 0), (0, 2)), ((1, 1), (1, 3), (1, 2)), mine, theirs, carried_sum,
        [(w_panels,), (z_plus,), (z_minus,), (other_a, other_b), (far_a, far_b)],
    )
    other_minus_a, other_plus_a = mark(SOME, other_minus_a, other_plus_a, limit=VMEM_LIMIT)
    send_b = after(other_b, total)
    send_far_b = after(far_b, other_far_a, total)
    other_minus_b = shift(send_b, "z", 1, NZ)
    other_plus_b = shift(send_b, "z", -1, NZ)
    other_far_b = shift(send_far_b, "y_lo", 1, 2)
    activated, slope = forward_late(
        late_x, total, cotangent, [other_plus_a, other_minus_a, other_far_a], "gelu_a"
    )
    last = (late_x, total, cotangent, [other_plus_b, other_minus_b, other_far_b], activated)
    blocks = [(w_panels,), (z_plus,), (far_a, far_b), (z_minus,), (other_a, other_b)]
    blocks += [(other_plus_a, other_plus_b), (other_far_a, other_far_b), (other_minus_a, other_minus_b)]

    half = tokens // 2
    m, t, slope, activated = gradient(((2, 0), (2, 1)), slope, blocks, "grad_far", last)
    far_sum = (m.astype(F32) + shift(t, "core", 1, 2).astype(F32)).astype(BF16)
    up, down = lax.optimization_barrier((far_sum[:, :half], far_sum[:, half:]))
    via_minus = shift(up, "x", 1, NX)
    via_plus = shift(down, "x", -1, NX)

    slope = after(slope, up, down)
    m, t = gradient(((1, 1), (3, 1)), slope, blocks, "grad_1")
    via_minus, via_plus = mark(DEAR, via_minus, via_plus)
    up, down = add_up(m, shift(t, "core", 1, 2), via_minus, via_plus, 1, [], "add_1")
    got_1 = shift(up, "x", 1, NX), shift(down, "x", -1, NX)

    slope = after(slope, up, down)
    m, t = gradient(((1, 0), (3, 0), (0, 1)), slope, blocks, "grad_0")
    got_1 = mark(DEAR, *got_1)
    up, down, to_other = add_up(m, shift(t, "core", 1, 2), via_minus, via_plus, 0, got_1, "add_0")
    got_0 = shift(up, "x", 1, NX), shift(down, "x", -1, NX)
    from_other = shift(to_other, "y_hi", 1, 2)

    slope = after(slope, up, down, to_other)
    m, t = gradient(((0, 0),), slope, blocks, "grad_own")
    got_0 = mark(DEAR, *got_0)
    from_other = mark(flops(60 * 10**9), from_other)[0]
    input_grad = m[0].astype(F32) + shift(t, "core", 1, 2)[0].astype(F32)
    for part in (*got_0, from_other):
        input_grad = input_grad + part.astype(F32)
    input_grad = input_grad.astype(BF16)
    return activated, input_grad.astype(BF16)


def solution(mesh):
    fine = Mesh(mesh.devices.reshape(2, 4, 4, 2, 2), ROWS_AXES + COLS_AXES)
    spec = P(ROWS_AXES, COLS_AXES)
    return jax.shard_map(
        body,
        mesh=fine,
        in_specs=(spec, spec, spec, spec),
        out_specs=(spec, spec),
        check_vma=False,
    )
```

```python
import jax
import jax.numpy as jnp
from jax import lax
from jax.experimental import pallas as pl
from jax.experimental.pallas import tpu as pltpu
from jax.sharding import Mesh, PartitionSpec as P

inv_root_two = 0.7071067811865476
inv_root_tau = 0.3989422804014327

NZ, NX = 4, 4
LANES = 256
WIDTH_A = 1280
ROWS_AXES = ("y_lo", "z")
COLS_AXES = ("x", "y_hi", "core")
F32, BF16 = jnp.float32, jnp.bfloat16
VMEM_LIMIT = 62 * 2**20
SMALL_LIMIT = 16 * 2**20
PARTS = 1
CHUNKS = 2


CHEAP = pl.CostEstimate(flops=1000, bytes_accessed=1000, transcendentals=0)


def flops(n):
    return pl.CostEstimate(flops=n, bytes_accessed=1000, transcendentals=0)


DEAR = flops(4 * 10**10)
SOME = flops(4 * 10**10)


def shift(value, axis, by, size):
    pairs = [(i, (i + by) % size) for i in range(size)]
    return lax.ppermute(value, axis, pairs)


def after(value, *deps):
    return lax.optimization_barrier((value, *deps))[0]


def panel_place(dy, dz):
    r = ((lax.axis_index("y_lo") + dy) & 1) * NZ + ((lax.axis_index("z") + dz) & (NZ - 1))
    dx = ((r >> 1) - lax.axis_index("x")) & (NX - 1)
    return (dx ^ (dx >> 1)) * 2 + ((r ^ lax.axis_index("y_hi")) & 1)


def block_place(dx, dyh):
    r = ((lax.axis_index("x") + dx) & (NX - 1)) * 2 + ((lax.axis_index("y_hi") + dyh) & 1)
    return (((r >> 2) ^ lax.axis_index("y_lo")) & 1) * NZ + ((r - lax.axis_index("z")) & (NZ - 1))


def forward_early(early, late, mine, theirs, start, shards):
    tokens, width = start.shape
    panels = sum(p.shape[0] for p in mine)
    n, n_p, n_late = len(shards), len(mine) + len(theirs), len(late)
    rows = shards[0][0].shape[0]
    pieces = [a for shard in shards for a in shard]

    def kernel(*refs):
        parts, (start_ref, *refs) = refs[:n_p], refs[n_p:]
        w_refs = refs[: len(pieces)]
        total_ref, late_x_ref, mine_ref, theirs_ref, sems, late_sems = refs[len(pieces) :]
        i = pl.program_id(0)
        own = lax.axis_index("core")
        out_copies = []
        for j, spot in enumerate(late):
            place = panel_place(*spot)
            for k, buf in enumerate((mine_ref, theirs_ref)):
                column = pl.multiple_of((2 * j + jnp.where(own == k, 0, 1)) * LANES, LANES)
                out_copies.append(
                    pltpu.make_async_copy(
                        buf.at[place],
                        late_x_ref.at[:, pl.ds(column, LANES)],
                        late_sems.at[2 * j + k],
                    )
                )

        @pl.when(i == 0)
        def _():
            copies = []
            for buf, own_parts in ((mine_ref, parts[: len(mine)]), (theirs_ref, parts[len(mine) :])):
                to = 0
                for part in own_parts:
                    held = buf.at[pl.ds(to, part.shape[0])]
                    copies.append(pltpu.make_async_copy(part, held, sems.at[len(copies)]))
                    to += part.shape[0]
            for c in copies:
                c.start()
            for c in copies:
                c.wait()
            for c in out_copies:
                c.start()

        lo = pl.multiple_of(own * LANES, LANES)
        hi = pl.multiple_of((1 - own) * LANES, LANES)
        lhs = jnp.concatenate(
            [r[panel_place(*spot)] for spot in early for r in (mine_ref, theirs_ref)], axis=1
        )
        rhs, at = [], 0
        for shard in shards:
            held = w_refs[at : at + len(shard)]
            for o in (lo, hi):
                block = held[0][pl.ds(o, LANES), :]
                if len(shard) == 2:
                    edge = shard[0].shape[1] // LANES
                    block = jnp.where(i < edge, block, held[1][pl.ds(o, LANES), :])
                rhs.append(block)
            at += len(shard)
        rhs = jnp.concatenate(rhs, axis=0)
        total_ref[...] = start_ref[...] + jnp.dot(lhs, rhs, preferred_element_type=F32)

        @pl.when(i == pl.num_programs(0) - 1)
        def _():
            for c in out_copies:
                c.wait()

    def piece_specs(shard):
        if len(shard) == 1:
            return [pl.BlockSpec((rows, LANES), lambda i, *_: (0, i))]
        edge = shard[0].shape[1] // LANES
        return [
            pl.BlockSpec((rows, LANES), lambda i, *_: (0, jnp.minimum(i, edge - 1))),
            pl.BlockSpec((rows, LANES), lambda i, *_: (0, jnp.maximum(i - edge, 0))),
        ]

    tile = pl.BlockSpec((tokens, LANES), lambda i, *_: (0, i))
    hbm = pl.BlockSpec(memory_space=pl.ANY)
    return pl.pallas_call(
        kernel,
        grid=(width // LANES,),
        in_specs=[hbm] * n_p + [tile] + [p for shard in shards for p in piece_specs(shard)],
        out_specs=[tile, hbm],
        scratch_shapes=[pltpu.VMEM((panels, tokens, LANES), BF16)] * 2
        + [pltpu.SemaphoreType.DMA((n_p,)), pltpu.SemaphoreType.DMA((2 * n_late,))],
        out_shape=[
            jax.ShapeDtypeStruct((tokens, width), F32),
            jax.ShapeDtypeStruct((tokens, 2 * n_late * LANES), BF16),
        ],
        compiler_params=pltpu.CompilerParams(vmem_limit_bytes=VMEM_LIMIT),
        cost_estimate=CHEAP,
        name="early",
    )(*mine, *theirs, start, *pieces)


def gelu(preact, cotangent):
    normal_cdf = 0.5 * (1.0 + lax.erf(preact * inv_root_two))
    normal_pdf = jnp.exp(-0.5 * preact * preact) * inv_root_tau
    slope = cotangent.astype(F32) * (normal_cdf + preact * normal_pdf)
    return (preact * normal_cdf).astype(BF16), slope.astype(BF16)


def forward_late(late_x, total, cotangent, shards, name):
    tokens, width = total.shape
    rows, cols = shards[0].shape
    n = len(shards)
    depth = late_x.shape[1]
    t = tokens // PARTS

    def kernel(x_ref, start_ref, cot_ref, *refs):
        w_refs, (act_ref, slope_ref) = refs[:n], refs[-2:]
        rhs = jnp.concatenate([w[...] for w in w_refs], axis=0)
        for p in range(PARTS):
            at = pl.ds(p * t, t)
            preact = start_ref[at, :] + jnp.dot(x_ref[at, :], rhs, preferred_element_type=F32)
            act_ref[at, :], slope_ref[at, :] = gelu(preact, cot_ref[at, :])

    tile = pl.BlockSpec((tokens, LANES), lambda i: (0, i))
    return pl.pallas_call(
        kernel,
        grid=(cols // LANES,),
        in_specs=[pl.BlockSpec((tokens, depth), lambda i: (0, 0)), tile, tile]
        + [pl.BlockSpec((rows, LANES), lambda i: (0, i))] * n,
        out_specs=[tile, tile],
        out_shape=[jax.ShapeDtypeStruct((tokens, width), BF16)] * 2,
        compiler_params=pltpu.CompilerParams(vmem_limit_bytes=VMEM_LIMIT),
        cost_estimate=CHEAP,
        name=name,
    )(late_x, total, cotangent, *shards)


def gradient(places, slope, blocks, name, last=None):
    tokens, width = slope.shape
    n_last = 0
    if last is not None:
        late_x, total, cotangent, shards, activated = last
        cols = shards[0].shape[1]
        edge = width - cols
        depth = late_x.shape[1]
        last_args = [late_x, total, cotangent, *shards, activated]
        n_last = len(last_args)
    rows = 2 * LANES
    n = len(places)
    arrays = [a for shard in blocks for a in shard]
    t = tokens // CHUNKS

    def kernel(s_hbm, *refs):
        last_refs, refs = refs[:n_last], refs[n_last:]
        a_refs, refs = refs[: len(arrays)], refs[len(arrays) :]
        mine_hbm, theirs_hbm, *refs = refs
        if last is not None:
            s_out, act_out, *refs = refs
            x_buf, total_buf, cot_buf, shard_buf, act_buf, *refs, l_sem, x_sem, act_sem = refs
        s_buf, w_buf, out_buf, s_sem, w_sem, out_sem = refs

        def fetch(k):
            wanted = block_place(*places[k])
            at = 0
            for j, shard in enumerate(blocks):
                held = a_refs[at : at + len(shard)]
                at += len(shard)

                @pl.when(wanted == j)
                def _():
                    to = 0
                    for ref in held:
                        w = ref.shape[1]
                        pltpu.make_async_copy(ref, w_buf.at[k, :, pl.ds(to, w)], w_sem.at[k]).start()
                        to += w

        chunks = [pl.ds(c * t, t) for c in range(CHUNKS)]
        had = width if last is None else edge
        loads = [
            pltpu.make_async_copy(
                s_hbm.at[at, pl.ds(0, had)], s_buf.at[at, pl.ds(0, had)], s_sem.at[c]
            )
            for c, at in enumerate(chunks)
        ]
        stores = []
        if last is None:
            fetch(0)
            for load in loads:
                load.start()
        else:
            x_hbm, total_hbm, cot_hbm, *shard_hbm = last_refs[:-1]
            tail = pl.ds(edge, cols)
            first = [
                pltpu.make_async_copy(ref, shard_buf.at[pl.ds(j * rows, rows)], l_sem.at[j])
                for j, ref in enumerate(shard_hbm)
            ]
            by_chunk = [
                [
                    pltpu.make_async_copy(x_hbm.at[at], x_buf.at[at], x_sem.at[0, c]),
                    pltpu.make_async_copy(total_hbm.at[at, tail], total_buf.at[at], x_sem.at[1, c]),
                    pltpu.make_async_copy(cot_hbm.at[at, tail], cot_buf.at[at], x_sem.at[2, c]),
                ]
                for c, at in enumerate(chunks)
            ]
            for load in first + sum(by_chunk, []):
                load.start()
            for load in loads:
                load.start()
            fetch(0)
            for load in first:
                load.wait()
            for c, at in enumerate(chunks):
                for load in by_chunk[c]:
                    load.wait()
                for b in range(cols // LANES):
                    here = pl.ds(b * LANES, LANES)
                    preact = total_buf[at, here] + jnp.dot(
                        x_buf[at, :], shard_buf[:, here], preferred_element_type=F32
                    )
                    act_buf[at, here], s_buf[at, pl.ds(edge + b * LANES, LANES)] = gelu(
                        preact, cot_buf[at, here]
                    )
                stores.append(pltpu.make_async_copy(act_buf.at[at], act_out.at[at, tail], act_sem.at[0, c]))
                stores.append(
                    pltpu.make_async_copy(s_buf.at[at, tail], s_out.at[at, tail], act_sem.at[1, c])
                )
                stores[-2].start()
                stores[-1].start()
        own = lax.axis_index("core")
        for k in range(n):
            if k + 1 < n:
                fetch(k + 1)
            pltpu.make_async_copy(a_refs[0], w_buf.at[k], w_sem.at[k]).wait()
            for c, at in enumerate(chunks):
                if k == 0:
                    loads[c].wait()
                for h, (half, out) in enumerate(((1 - own, theirs_hbm), (own, mine_hbm))):
                    part = w_buf[k, pl.ds(pl.multiple_of(half * LANES, LANES), LANES), :]
                    out_buf[k, h, at, :] = lax.dot_general(
                        s_buf[at, :], part, (((1,), (1,)), ((), ())), preferred_element_type=F32
                    ).astype(BF16)
                    store = pltpu.make_async_copy(
                        out_buf.at[k, h, at], out.at[k, at], out_sem.at[k, h, c]
                    )
                    store.start()
                    stores.append(store)
        for store in stores:
            store.wait()

    last_scratch, last_sems, last_out, aliases = [], [], [], {}
    if last is not None:
        last_scratch = [
            pltpu.VMEM((tokens, depth), BF16),
            pltpu.VMEM((tokens, cols), F32),
            pltpu.VMEM((tokens, cols), BF16),
            pltpu.VMEM((depth, cols), BF16),
            pltpu.VMEM((tokens, cols), BF16),
        ]
        last_sems = [
            pltpu.SemaphoreType.DMA((len(shards),)),
            pltpu.SemaphoreType.DMA((3, CHUNKS)),
            pltpu.SemaphoreType.DMA((2, CHUNKS)),
        ]
        last_out = [jax.ShapeDtypeStruct((tokens, width), BF16)] * 2
        aliases = {0: 2, n_last: 3}
    hbm = pl.BlockSpec(memory_space=pl.ANY)
    return pl.pallas_call(
        kernel,
        in_specs=[hbm] * (1 + n_last + len(arrays)),
        out_specs=[hbm] * (2 + len(last_out)),
        scratch_shapes=last_scratch
        + [
            pltpu.VMEM((tokens, width), BF16),
            pltpu.VMEM((n, rows, width), BF16),
            pltpu.VMEM((n, 2, tokens, LANES), BF16),
            pltpu.SemaphoreType.DMA((CHUNKS,)),
            pltpu.SemaphoreType.DMA((n,)),
            pltpu.SemaphoreType.DMA((n, 2, CHUNKS)),
        ]
        + last_sems,
        out_shape=[jax.ShapeDtypeStruct((n, tokens, LANES), BF16)] * 2 + last_out,
        input_output_aliases=aliases,
        compiler_params=pltpu.CompilerParams(vmem_limit_bytes=VMEM_LIMIT),
        cost_estimate=CHEAP,
        name=name,
    )(slope, *(last_args if last is not None else []), *arrays)


def mark(cost, *arrays, limit=SMALL_LIMIT):
    n = len(arrays)
    any_space = [pl.BlockSpec(memory_space=pl.ANY)] * n
    return pl.pallas_call(
        lambda *refs: None,
        in_specs=any_space,
        out_specs=any_space,
        out_shape=[jax.ShapeDtypeStruct(a.shape, a.dtype) for a in arrays],
        input_output_aliases={i: i for i in range(n)},
        compiler_params=pltpu.CompilerParams(vmem_limit_bytes=limit),
        cost_estimate=cost,
        name="mark",
    )(*arrays)


def add_up(mine, back, via_minus, via_plus, dyh, got, name):
    tokens, lanes = mine.shape[1:]
    steps = 2
    t = tokens // steps

    def kernel(mine_ref, back_ref, minus_ref, plus_ref, *refs):
        got_refs, (up_ref, down_ref, *own_ref) = refs[: len(got)], refs[len(got) :]
        first = pl.program_id(0) < steps // 2
        total = mine_ref[...].astype(F32) + back_ref[...].astype(F32)
        minus, plus = minus_ref[0].astype(F32), plus_ref[0].astype(F32)
        up_ref[...] = (total[0] + jnp.where(first, minus, 0.0)).astype(BF16)
        down_ref[...] = (total[1] + jnp.where(first, 0.0, plus)).astype(BF16)
        if got:
            own = total[2]
            for ref in got_refs:
                own = own + ref[...].astype(F32)
            own_ref[0][...] = own.astype(BF16)

    tile = pl.BlockSpec((t, lanes), lambda i: (i, 0))
    stack = pl.BlockSpec((mine.shape[0], t, lanes), lambda i: (0, i, 0))
    last = steps // 2 - 1
    n_out = 3 if got else 2
    return pl.pallas_call(
        kernel,
        grid=(steps,),
        in_specs=[
            stack,
            stack,
            pl.BlockSpec((1, t, lanes), lambda i: (dyh, jnp.minimum(i, last), 0)),
            pl.BlockSpec((1, t, lanes), lambda i: (dyh, jnp.maximum(i - last - 1, 0), 0)),
        ]
        + [tile] * len(got),
        out_specs=[tile] * n_out,
        out_shape=[jax.ShapeDtypeStruct((tokens, lanes), BF16)] * n_out,
        compiler_params=pltpu.CompilerParams(vmem_limit_bytes=SMALL_LIMIT),
        cost_estimate=CHEAP,
        name=name,
    )(mine, back, via_minus, via_plus, *got)


def body(carried_sum, x_panels, w_panels, cotangent):
    tokens, width = carried_sum.shape
    width_a = WIDTH_A
    rows = w_panels.shape[0]

    w_a, w_b = w_panels[:, :width_a], w_panels[:, width_a:]
    z_minus = shift(w_panels, "z", 1, NZ)
    z_plus = shift(w_panels, "z", -1, NZ)
    other_a = shift(w_a, "y_lo", 1, 2)
    pair = mark(flops(38 * 10**9), jnp.stack([x_panels, shift(x_panels, "y_hi", 1, 2)]))[0]
    x_minus = shift(pair, "x", 1, NX)
    x_plus = shift(pair, "x", -1, NX)
    z_minus, z_plus = mark(flops(80 * 10**9), z_minus, z_plus)
    other_a = mark(DEAR, other_a)[0]
    up, down = z_minus[: rows // 2], z_plus[rows // 2 :]
    up, down, w_b, other_a, x_minus, x_plus = lax.optimization_barrier(
        (up, down, w_b, other_a, x_minus, x_plus)
    )
    far_top = shift(up, "z", 1, NZ)
    far_low = shift(down, "z", -1, NZ)
    other_b = shift(w_b, "y_lo", 1, 2)
    x_far = [shift(x_minus[0], "x", 1, NX), shift(x_plus[1], "x", -1, NX)]
    x_far = jnp.stack(x_far)
    near = jnp.concatenate([pair, x_plus, x_minus])
    far_a = jnp.concatenate([far_top[:, :width_a], far_low[:, :width_a]])
    far_b = jnp.concatenate([far_top[:, width_a:], far_low[:, width_a:]])
    send_a, near, x_far = lax.optimization_barrier(
        (other_a, near, x_far, far_top, far_low, other_b)
    )[:3]
    mine = [pair, x_plus, x_minus, x_far]
    theirs = [shift(near, "core", 1, 2), shift(x_far, "core", 1, 2)]
    other_minus_a = shift(send_a, "z", 1, NZ)
    other_plus_a = shift(send_a, "z", -1, NZ)
    other_far_a = shift(far_a, "y_lo", 1, 2)
    total, late_x = forward_early(
        ((0, 0), (0, 1), (0, 3), (1, 0), (0, 2)), ((1, 1), (1, 3), (1, 2)), mine, theirs, carried_sum,
        [(w_panels,), (z_plus,), (z_minus,), (other_a, other_b), (far_a, far_b)],
    )
    other_minus_a, other_plus_a = mark(SOME, other_minus_a, other_plus_a, limit=VMEM_LIMIT)
    send_b = after(other_b, total)
    send_far_b = after(far_b, other_far_a, total)
    other_minus_b = shift(send_b, "z", 1, NZ)
    other_plus_b = shift(send_b, "z", -1, NZ)
    other_far_b = shift(send_far_b, "y_lo", 1, 2)
    activated, slope = forward_late(
        late_x, total, cotangent, [other_plus_a, other_minus_a, other_far_a], "gelu_a"
    )
    last = (late_x, total, cotangent, [other_plus_b, other_minus_b, other_far_b], activated)
    blocks = [(w_panels,), (z_plus,), (far_a, far_b), (z_minus,), (other_a, other_b)]
    blocks += [(other_plus_a, other_plus_b), (other_far_a, other_far_b), (other_minus_a, other_minus_b)]

    half = tokens // 2
    m, t, slope, activated = gradient(((2, 0), (2, 1)), slope, blocks, "grad_far", last)
    far_sum = (m.astype(F32) + shift(t, "core", 1, 2).astype(F32)).astype(BF16)
    up, down = lax.optimization_barrier((far_sum[:, :half], far_sum[:, half:]))
    via_minus = shift(up, "x", 1, NX)
    via_plus = shift(down, "x", -1, NX)

    slope = after(slope, up, down)
    m, t = gradient(((1, 1), (3, 1)), slope, blocks, "grad_1")
    via_minus, via_plus = mark(DEAR, via_minus, via_plus)
    up, down = add_up(m, shift(t, "core", 1, 2), via_minus, via_plus, 1, [], "add_1")
    got_1 = shift(up, "x", 1, NX), shift(down, "x", -1, NX)

    slope = after(slope, up, down)
    m, t = gradient(((1, 0), (3, 0), (0, 1)), slope, blocks, "grad_0")
    got_1 = mark(DEAR, *got_1)
    up, down, to_other = add_up(m, shift(t, "core", 1, 2), via_minus, via_plus, 0, got_1, "add_0")
    got_0 = shift(up, "x", 1, NX), shift(down, "x", -1, NX)
    from_other = shift(to_other, "y_hi", 1, 2)

    slope = after(slope, up, down, to_other)
    m, t = gradient(((0, 0),), slope, blocks, "grad_own")
    got_0 = mark(DEAR, *got_0)
    from_other = mark(flops(60 * 10**9), from_other)[0]
    input_grad = m[0].astype(F32) + shift(t, "core", 1, 2)[0].astype(F32)
    for part in (*got_0, from_other):
        input_grad = input_grad + part.astype(F32)
    input_grad = input_grad.astype(BF16)
    return activated, input_grad.astype(BF16)


def solution(mesh):
    fine = Mesh(mesh.devices.reshape(2, 4, 4, 2, 2), ROWS_AXES + COLS_AXES)
    spec = P(ROWS_AXES, COLS_AXES)
    return jax.shard_map(
        body,
        mesh=fine,
        in_specs=(spec, spec, spec, spec),
        out_specs=(spec, spec),
        check_vma=False,
    )
```
